32 devices in a mesh: tm: 2 (over x), chan: 16 (over z, y, core).
Axes of the slice: x: 2, y: 2, z: 4, core: 2. Of those that a mesh axis runs over, the one named last changes fastest.
Arguments:
- voltage_frequency_samples: bfloat16 [2, 64, 30, 2, 8192], P(None, ('tm', 'chan')), may hold values from -6 to 6
- lag_lookup_entry: int32 [2, 2, 30], P('tm'), may hold values from 0 to 63
- lag_lookup_turning: float32 [64, 8192], P(None, 'chan'), may hold values from -3.140625 to 3.140625
- antenna_pair_members: int32 [435, 2], replicated, may hold values from 0 to 29, as said below
- frequency_bin_target: int32 [8192], P('chan'), may hold values from 0 to 63, as said below
Outputs:
- centre_vis: float32 [128, 2, 4, 435], P(('tm', 'chan'))
The draws below stay inside these ranges and needn't reach their ends.
Inputs may be any that keep to these rules, and one draw needn't show every extreme that they name: `antenna_pair_members`: every unordered pair of two different stations of the 30 appears in exactly one row, in either order. `frequency_bin_target`: each of the 64 output channels receives exactly 128 fine channels.
All inputs are finite; a program needn't handle non-finite values.
Results may differ from the reference program's by a relative error of at most 0.0029.
Values may be sent and summed in bfloat16 or wider, within the bound.
No kernel may reach another device: no remote copies, remote signals or barrier semaphores. Data moves between devices by JAX's collectives and lax.ppermute only.
A program may use at most 128 MiB of HBM per device.

```python
import jax
import jax.numpy as jnp
import numpy as np
from jax import lax

S = 30
POL = 2
F = 8192
Q = 64
K = 64
C = 2
B = 435
SPECTRA = 64
SUBINTEGRATIONS = 2


def draw_antenna_pair_members(key, part):
    lower_np, upper_np = np.triu_indices(S, 1)
    station_pairs = jnp.stack([jnp.asarray(lower_np, jnp.int32), jnp.asarray(upper_np, jnp.int32)], axis=1)
    shuffle = jax.random.permutation(jax.random.fold_in(key, 11), B)
    station_pairs = station_pairs[shuffle]
    swapped = jax.random.randint(jax.random.fold_in(key, 12), (B,), 0, 2)
    return jnp.where(swapped[:, None] == 1, station_pairs[:, ::-1], station_pairs).astype(jnp.int32)


def draw_frequency_bin_target(key, part):
    shuffle = jax.random.permutation(jax.random.fold_in(key, 21), F)
    return (shuffle % Q).astype(jnp.int32)


def with_ends(result, own_key, least, top_value):
    extent = result.shape
    spot = [jax.random.randint(jax.random.fold_in(own_key, axis), (), 0, extent[axis]) for axis in range(len(extent))]
    result = result.at[tuple(spot)].set(least)
    longest = extent.index(max(extent))
    spot[longest] = (spot[longest] + 1) % extent[longest]
    return result.at[tuple(spot)].set(top_value)


def block_levels(own_key, shape, cuts, least, high):
    loudness = 1.0
    for dim, shards_of in cuts:
        heights = jax.random.uniform(jax.random.fold_in(jax.random.fold_in(own_key, 6), dim), (shards_of,), jnp.float32, least / len(cuts), high / len(cuts))
        loudness = loudness * jnp.repeat(jnp.exp(heights), shape[dim] // shards_of).reshape((-1,) + (1,) * (len(shape) - 1 - dim))
    return loudness


def scatter_about(stream_key, dims, width, bound, shards=(), held_as=jnp.bfloat16):
    array = jax.random.normal(stream_key, dims, jnp.float32) * width
    if len(shards) > 0:
        array = block_levels(stream_key, dims, shards, -0.22, 0.18) * array
    return jnp.clip(array, min=-bound, max=bound).astype(held_as)


def setup_inputs(seed: int = 0) -> dict:
    streams_of = jax.random.split(jax.random.key(seed), 6)
    return {
        "voltage_frequency_samples": scatter_about(streams_of[0], (2, SPECTRA, S, POL, F), 1.0, 6.0, ((1, 32),)),
        "lag_lookup_entry": with_ends(jax.random.randint(streams_of[1], (SUBINTEGRATIONS, C, S), 0, K), jax.random.fold_in(streams_of[1], 1), 0, K - 1).astype(jnp.int32),
        "lag_lookup_turning": jnp.clip(jax.random.uniform(streams_of[2], (K, F), jnp.float32, -3.140625, 3.140625), -3.140625, 3.140625),
        "antenna_pair_members": draw_antenna_pair_members(jax.random.fold_in(streams_of[5], 71), 0),
        "frequency_bin_target": draw_frequency_bin_target(jax.random.fold_in(streams_of[5], 71), 0),
    }


def reference(voltage_frequency_samples, lag_lookup_entry, lag_lookup_turning, antenna_pair_members, frequency_bin_target):
    per_group = SPECTRA // SUBINTEGRATIONS
    left_antenna_number = antenna_pair_members[:, 0]
    right_antenna_number = antenna_pair_members[:, 1]

    def correlate(left_part, right_part):
        return jnp.einsum("taf,tbf->abf", left_part.astype(jnp.float32), right_part.astype(jnp.float32))

    def one_group(carry, group):
        block = lax.dynamic_slice_in_dim(voltage_frequency_samples, (group * per_group).astype(jnp.int32), per_group, axis=1)
        real_part = block[0].reshape(per_group, S * POL, F)
        imag_part = block[1].reshape(per_group, S * POL, F)
        vis_real = correlate(real_part, real_part) + correlate(imag_part, imag_part)
        vis_imag = correlate(imag_part, real_part) - correlate(real_part, imag_part)
        vis_real = vis_real.reshape(S, POL, S, POL, F)[left_antenna_number, :, right_antenna_number].reshape(B, POL * POL, F)
        vis_imag = vis_imag.reshape(S, POL, S, POL, F)[left_antenna_number, :, right_antenna_number].reshape(B, POL * POL, F)
        phases = jnp.take(lag_lookup_turning, lag_lookup_entry[group], axis=0)
        phase_diff = phases[:, left_antenna_number] - phases[:, right_antenna_number]

        def rotate_one(angles):
            cosine = jnp.cos(angles)[:, None, :]
            sine = jnp.sin(angles)[:, None, :]
            rot_real = (vis_real * cosine + vis_imag * sine).astype(jnp.bfloat16)
            rot_imag = (vis_imag * cosine - vis_real * sine).astype(jnp.bfloat16)
            sum_real = jax.ops.segment_sum(jnp.moveaxis(rot_real.astype(jnp.float32), 2, 0), frequency_bin_target, num_segments=Q)
            sum_imag = jax.ops.segment_sum(jnp.moveaxis(rot_imag.astype(jnp.float32), 2, 0), frequency_bin_target, num_segments=Q)
            return jnp.stack([jnp.transpose(sum_real, (0, 2, 1)), jnp.transpose(sum_imag, (0, 2, 1))], axis=1)

        return carry + lax.map(rotate_one, phase_diff), None

    start = jnp.zeros((C, Q, 2, POL * POL, B), jnp.float32)
    total, _ = lax.scan(one_group, start, jnp.arange(SUBINTEGRATIONS, dtype=jnp.int32))
    return (total * (Q / F)).reshape(C * Q, 2, POL * POL, B)
```

```python
import functools

import jax
import jax.numpy as jnp
import numpy as np
from jax import lax
from jax.experimental import pallas as pl
from jax.experimental.pallas import tpu as pltpu
from jax.sharding import Mesh
from jax.sharding import PartitionSpec as P

Q = 64
LANES = 128
HALF = 64
ROW = 8
GROUP = 2
TURN = 65536.0
COSINE = (-0.9999992251396179, 19.738981246948242, -64.92865753173828, 85.27162170410156, -58.79049301147461, 21.07110595703125)
VMEM = pl.BlockSpec(memory_space=pltpu.VMEM)
SMEM = pl.BlockSpec(memory_space=pltpu.SMEM)
ANY = pl.BlockSpec(memory_space=pl.ANY)


def iota(shape, dim):
    return lax.broadcasted_iota(jnp.int32, shape, dim)


def params(mib):
    return pltpu.CompilerParams(vmem_limit_bytes=mib * 1024 * 1024)


def pack_kernel(turning_ref, bins_ref, out_ref):
    entries, fine = turning_ref.shape
    rows = fine // 2
    codes = jnp.round(turning_ref[...] * (TURN / (2.0 * np.pi)))
    flipped = codes.T
    pair = jnp.concatenate([flipped[:rows], flipped[rows:]], axis=1)
    out_ref[0:rows, :] = pair.astype(jnp.int32).astype(jnp.int16)
    spare = jnp.zeros((out_ref.shape[0] - rows - bins_ref.shape[0], LANES), jnp.int32)
    out_ref[rows:, :] = jnp.concatenate([bins_ref[...], spare], axis=0).astype(jnp.int16)


def encode(block):
    top = jnp.max(jnp.max(jnp.abs(block), axis=0, keepdims=True), axis=1, keepdims=True)
    power = jnp.floor(jnp.log2(jnp.maximum(top, 1e-30)))
    code = jnp.clip(jnp.round(block * jnp.exp2(14.0 - power)), -32767.0, 32767.0)
    code = jnp.where(iota(block.shape, 0) == 60, power, code)
    return code.astype(jnp.int32).astype(jnp.int16)


def decode(code):
    code = code.astype(jnp.int32).astype(jnp.float32)
    scale = jnp.exp2(code[60:61, 0:1] - 14.0)
    return code * scale


def correlate_kernel(
    place_ref, own_ref, other_ref, entry_ref, *rest, chips, near, far, pairs, spectra, fine
):
    blocks = rest[: 2 * chips]
    outs = rest[2 * chips : 2 * chips + GROUP * near]
    held, raw, even, odd, source_v, source_s, sems, source_sem = rest[2 * chips + GROUP * near :]
    chip = place_ref[0]
    core = place_ref[1]
    slots = raw.shape[1]
    q_here = 2 * far * near * pairs

    def fetch(side, slot):
        ref = (own_ref, other_ref)[side]
        return pltpu.make_async_copy(
            ref.at[:, :, :, :, pl.ds(pl.multiple_of(slot * LANES, LANES), LANES)],
            raw.at[side, slot, :, :, pl.ds(0, ref.shape[2])],
            sems.at[side, slot],
        )

    def start(slot, _):
        for side in range(2):
            raw[side, slot, :, :, 30:32] = jnp.zeros((2, spectra, 2, 2, LANES), jnp.bfloat16)
            fetch(side, slot).start()
        return 0

    lax.fori_loop(0, slots, start, 0)

    above = (iota((fine, fine), 0) < iota((fine, fine), 1)).astype(jnp.bfloat16)
    carry = jnp.zeros((q_here, 1), jnp.float32)
    found = jnp.zeros((2 * q_here, LANES), jnp.float32)
    bases = []
    for index in range(2 * chips):
        owner = (chip ^ (index % chips)) * 2 + (core if index < chips else 1 - core)
        bases.append(owner * fine)
        rows = blocks[index][fine // 2 : fine // 2 + 16, :].astype(jnp.int32)
        bins = jnp.concatenate([rows[r : r + 1, :] for r in range(fine // LANES)], axis=1)
        per = 2 * pairs
        bin_owner = bins // per
        relative = (bin_owner // 2) ^ chip
        label = ((relative % near) * far + relative // near) * per + bins % per
        label = jnp.where(bin_owner % 2 == core, label, -1)
        hit = iota((q_here, fine), 0) == label
        hit_b = hit.astype(jnp.bfloat16)
        before = jnp.dot(hit_b, above, preferred_element_type=jnp.float32)
        rank = jnp.sum(jnp.where(hit, before + carry, 0.0), axis=0, keepdims=True)
        carry = carry + before[:, fine - 1 : fine] + hit_b[:, fine - 1 : fine].astype(jnp.float32)
        at_rank = (iota((LANES, fine), 0) == rank.astype(jnp.int32)).astype(jnp.bfloat16)
        lane = iota((q_here, fine), 1)
        high = jnp.where(hit, owner * (fine // LANES) + lane // LANES, 0)
        low = jnp.where(hit, lane % LANES, 0)
        ids = jnp.concatenate([high, low], axis=0).astype(jnp.float32).astype(jnp.bfloat16)
        found = found + lax.dot_general(
            ids, at_rank, (((1,), (1,)), ((), ())), preferred_element_type=jnp.float32
        )
    source_v[...] = ((found[:q_here] * LANES + found[q_here:]) * ROW).astype(jnp.int32)
    to_scalar = pltpu.make_async_copy(source_v, source_s, source_sem)
    to_scalar.start()

    row = iota((2 * LANES, LANES), 0)
    weight = jnp.where(row < LANES, 2.0**-8, 2.0**-16)
    columns = []
    for half in range(2):
        for centre in range(GROUP):
            wanted = entry_ref[centre : centre + 1, :]
            match = (row % HALF == wanted) & ((row // HALF) % 2 == half)
            columns.append(jnp.where(match, weight, 0.0).astype(jnp.bfloat16))
    spread = jnp.concatenate(columns, axis=1)
    for index in range(2 * chips):
        code = blocks[index][0 : fine // 2, :].astype(jnp.int32).astype(jnp.float32)
        high = jnp.floor(code * (1.0 / 256.0))
        low = code - 256.0 * high
        digits = jnp.concatenate([high, low], axis=1).astype(jnp.bfloat16)
        turns = jnp.dot(digits, spread, preferred_element_type=jnp.float32)
        for half in range(2):
            for centre in range(GROUP):
                column = (half * GROUP + centre) * LANES
                first = (bases[index] + half * (fine // 2)) * ROW + 2 * spectra + centre
                held[pl.ds(first, fine // 2, stride=ROW), :] = turns[:, column : column + LANES]

    eye = (iota((2 * LANES, 2 * LANES), 0) == iota((2 * LANES, 2 * LANES), 1)).astype(jnp.bfloat16)

    def flip(step, _):
        for side in range(2):
            for unit in range(2):
                slot = step * 4 + unit * 2
                fetch(side, slot).wait()
                fetch(side, slot + 1).wait()
                parts = []
                for k in range(2):
                    block = raw[side, slot + k].reshape(2 * spectra * HALF, LANES)
                    parts.append(
                        jnp.concatenate(
                            [
                                block[(part * spectra + t) * HALF : (part * spectra + t + 1) * HALF]
                                for t in range(spectra)
                                for part in range(2)
                            ],
                            axis=0,
                        )
                    )
                flat = jnp.concatenate(parts, axis=1)
                tall = lax.dot_general(
                    eye, flat, (((1,), (1,)), ((), ())), preferred_element_type=jnp.float32
                )
                for t in range(spectra):
                    first = slot * LANES * ROW + side * spectra + t
                    held[pl.ds(first, 2 * LANES, stride=ROW), :] = tall[:, t * LANES : (t + 1) * LANES]
        return 0

    lax.fori_loop(0, slots // 4, flip, 0)
    to_scalar.wait()

    def gather(pair, into):
        for unit in range(2):
            for first in range(0, LANES, 32):
                at = [source_s[2 * pair + unit, first + k] for k in range(32)]
                rows = [held[pl.ds(pl.multiple_of(a, ROW), ROW), :] for a in at]
                for k in range(32):
                    into[pl.ds((unit * LANES + first + k) * ROW, ROW), :] = rows[k]

    lane = iota((LANES, LANES), 1)
    left = lane < HALF
    quarter = jnp.where(left, 0.0, 0.25)
    upper = (iota((HALF, LANES), 1) % HALF) > iota((HALF, LANES), 0)
    left_h = iota((HALF, LANES), 1) < HALF

    def compute(held_rows):
        packed = [[], []]
        for unit in range(2):
            base = unit * LANES * ROW
            volts = [held_rows[pl.ds(base + t, LANES, stride=ROW), :] for t in range(2 * spectra)]
            swapped = [pltpu.roll(v, HALF, 1) for v in volts]
            for centre in range(GROUP):
                turns = held_rows[pl.ds(base + 2 * spectra + centre, LANES, stride=ROW), :]
                z = jnp.abs(turns - quarter) - 0.5
                z = z * z
                wave = jnp.full_like(z, COSINE[-1])
                for coefficient in COSINE[-2::-1]:
                    wave = wave * z + coefficient
                turned = pltpu.roll(wave, HALF, 1)
                cosine = jnp.where(left, wave, turned)
                sine = jnp.where(left, turned, -wave)
                rotated = jnp.concatenate(
                    [v * cosine + s * sine for v, s in zip(volts, swapped)], axis=0
                )
                coarse = rotated.astype(jnp.bfloat16)
                rest_of = (rotated - coarse.astype(jnp.float32)).astype(jnp.bfloat16)
                both = jnp.concatenate([coarse, rest_of], axis=1)
                product = lax.dot_general(
                    coarse, both, (((0,), (0,)), ((), ())), preferred_element_type=jnp.float32
                )
                product = product[:, :LANES] + product[:, LANES:]
                under = pltpu.roll(product[HALF:], HALF, 1)
                packed[centre].append(product[:HALF] + jnp.where(left_h, under, -under))
        results = []
        for centre in range(GROUP):
            first, second = packed[centre]
            first = jnp.where(upper, first, pltpu.roll(first, HALF, 1))
            second = jnp.where(upper, pltpu.roll(second, HALF, 1), second)
            results.append(jnp.where(left_h, first, second))
        return results

    def store(out_ref, at, value):
        if out_ref.dtype == jnp.int16:
            value = encode(value)
        out_ref[pl.ds(pl.multiple_of(at * HALF, HALF), HALF), :] = value

    each = far * pairs
    last = near * each - 1
    gather(0, even)
    for y in range(near):

        def two(step, _):
            pair = y * each + 2 * step
            gather(jnp.minimum(pair + 1, last), odd)
            for centre, value in enumerate(compute(even)):
                store(outs[centre * near + y], 2 * step, value)
            gather(jnp.minimum(pair + 2, last), even)
            for centre, value in enumerate(compute(odd)):
                store(outs[centre * near + y], 2 * step + 1, value)
            return 0

        lax.fori_loop(0, each // 2, two, 0)


def merge_kernel(own_ref, *refs, arrivals, far, pairs):
    own_out = refs[arrivals]
    outs = refs[arrivals + 1 :]
    for z in range(far):
        for pair in range(pairs):
            at = pl.ds((z * pairs + pair) * HALF, HALF)
            total = own_ref[at, :]
            for ref in refs[:arrivals]:
                total = total + decode(ref[at, :])
            to = pl.ds(pair * HALF, HALF)
            if z == 0:
                own_out[to, :] = total
            else:
                outs[z - 1][to, :] = encode(total)


def finish_kernel(members_ref, own_ref, *refs, arrivals, pairs, scale):
    out_ref = refs[arrivals]
    baselines = members_ref.shape[1]
    first = members_ref[0:1, :]
    second = members_ref[1:2, :]
    rising = first < second
    station = iota((HALF, baselines), 0)
    for pair in range(pairs):
        at = pl.ds(pair * HALF, HALF)
        total = own_ref[at, :]
        for ref in refs[:arrivals]:
            total = total + decode(ref[at, :])
        total = total * scale
        total = jnp.where(iota(total.shape, 0) < 60, total, 0.0)
        flipped = total.T
        coarse = flipped.astype(jnp.bfloat16)
        medium = (flipped - coarse.astype(jnp.float32)).astype(jnp.bfloat16)
        fine = (flipped - coarse.astype(jnp.float32) - medium.astype(jnp.float32)).astype(jnp.bfloat16)
        stack = jnp.concatenate([coarse, medium, fine], axis=0)
        picked = {}
        for side, members in enumerate((first, second)):
            for p in range(2):
                choose = (station == 2 * members + p).astype(jnp.bfloat16)
                rows = jnp.dot(stack, choose, preferred_element_type=jnp.float32)
                rows = rows[:LANES] + rows[LANES : 2 * LANES] + rows[2 * LANES :]
                partner = second if side == 0 else first
                for half in range(2):
                    for p2 in range(2):
                        match = station == 2 * partner + p2
                        part = rows[half * HALF : (half + 1) * HALF]
                        picked[side, half, p, p2] = jnp.sum(
                            jnp.where(match, part, 0.0), axis=0, keepdims=True
                        )
        for half in range(2):
            real, imaginary = [], []
            for p in range(2):
                for p2 in range(2):
                    a = picked[0, half, p, p2]
                    b = picked[1, half, p2, p]
                    real.append(jnp.where(rising, a, b))
                    imaginary.append(jnp.where(rising, b, -a))
            out_ref[2 * pair + half, 0] = jnp.concatenate(real, axis=0)
            out_ref[2 * pair + half, 1] = jnp.concatenate(imaginary, axis=0)


def on_device(volts, entry, turning, members, target, *, tm, chips):
    near = max(1, chips // 4)
    far = chips // near
    fine = turning.shape[1]
    spectra = volts.shape[1]
    centres = entry.shape[1]
    per_device = Q // (2 * chips)
    pairs = per_device // 2
    channels = volts.shape[4]

    def across_chips(x, step):
        return lax.ppermute(x, "chip", [(i, i ^ step) for i in range(chips)])

    def across_cores(x):
        return lax.ppermute(x, "core", [(0, 1), (1, 0)])

    other = across_cores(volts)
    block = pl.pallas_call(
        pack_kernel,
        in_specs=[VMEM, VMEM],
        out_specs=VMEM,
        out_shape=jax.ShapeDtypeStruct((fine // 2 + 16, LANES), jnp.int16),
        name="pack",
    )(turning, target.reshape(fine // LANES, LANES))
    gathered = {0: block}
    step = chips // 2
    while step:
        for known in list(gathered):
            gathered[known ^ step] = across_chips(gathered[known], step)
        step //= 2
    mine = [gathered[k] for k in range(chips)]
    theirs = [across_cores(x) for x in mine]

    chip = lax.axis_index("chip")
    core = lax.axis_index("core")
    x = lax.axis_index("tm")
    place = jnp.stack([chip, core]).astype(jnp.int32)
    order = jnp.arange(centres, dtype=jnp.int32) ^ x
    lanes = jnp.repeat(entry[0], 2, axis=1)
    lanes = jnp.pad(lanes, ((0, 0), (0, HALF - lanes.shape[1])), constant_values=-1)
    lanes = jnp.concatenate([lanes, lanes], axis=1)
    lanes = jnp.take(lanes, order, axis=0)

    sums = {}
    for first in range(0, centres, GROUP):
        kinds = [
            jnp.float32 if first + c == 0 and y == 0 else jnp.int16
            for c in range(GROUP)
            for y in range(near)
        ]
        results = pl.pallas_call(
            functools.partial(
                correlate_kernel,
                chips=chips,
                near=near,
                far=far,
                pairs=pairs,
                spectra=spectra,
                fine=fine,
            ),
            in_specs=[SMEM, ANY, ANY, VMEM] + [VMEM] * (2 * chips),
            out_specs=[VMEM] * (GROUP * near),
            out_shape=[
                jax.ShapeDtypeStruct((far * pairs * HALF, LANES), kind) for kind in kinds
            ],
            scratch_shapes=[
                pltpu.VMEM((channels * ROW, LANES), jnp.float32),
                pltpu.VMEM((2, channels // LANES, 2, spectra, 32, 2, LANES), jnp.bfloat16),
                pltpu.VMEM((2 * LANES * ROW, LANES), jnp.float32),
                pltpu.VMEM((2 * LANES * ROW, LANES), jnp.float32),
                pltpu.VMEM((Q // 2, LANES), jnp.int32),
                pltpu.SMEM((Q // 2, LANES), jnp.int32),
                pltpu.SemaphoreType.DMA((2, channels // LANES)),
                pltpu.SemaphoreType.DMA,
            ],
            compiler_params=params(58),
            name="correlate",
        )(place, volts, other, lanes[first : first + GROUP], *mine, *theirs)
        for c in range(GROUP):
            for y in range(near):
                sums[first + c, y] = results[c * near + y]

    flat = [(a, b) for a in range(tm) for b in range(chips)]
    arrived = []
    for c in range(centres):
        for y in range(near):
            if c or y:
                route = [(a * chips + b, (a ^ c) * chips + (b ^ y)) for a, b in flat]
                arrived.append(lax.ppermute(sums[c, y], ("tm", "chip"), route))
    rows = pairs * HALF
    merged = pl.pallas_call(
        functools.partial(merge_kernel, arrivals=len(arrived), far=far, pairs=pairs),
        in_specs=[VMEM] * (1 + len(arrived)),
        out_specs=[VMEM] * far,
        out_shape=[
            jax.ShapeDtypeStruct((rows, LANES), jnp.int16 if z else jnp.float32)
            for z in range(far)
        ],
        name="merge",
    )(sums[0, 0], *arrived)
    final = [across_chips(merged[z], z * near) for z in range(1, far)]
    return pl.pallas_call(
        functools.partial(finish_kernel, arrivals=len(final), pairs=pairs, scale=Q / channels),
        in_specs=[VMEM] * (2 + len(final)),
        out_specs=VMEM,
        out_shape=jax.ShapeDtypeStruct((per_device, 2, 4, members.shape[0]), jnp.float32),
        name="finish",
    )(members.T, merged[0], *final)


def solution(mesh):
    tm = mesh.shape["tm"]
    chips = mesh.shape["chan"] // 2
    inner = Mesh(mesh.devices.reshape(tm, chips, 2), ("tm", "chip", "core"))
    every = ("tm", "chip", "core")
    split = ("chip", "core")
    return jax.shard_map(
        functools.partial(on_device, tm=tm, chips=chips),
        mesh=inner,
        in_specs=(
            P(None, every, None, None, None),
            P("tm", None, None),
            P(None, split),
            P(),
            P(split),
        ),
        out_specs=P(every, None, None, None),
        check_vma=False,
    )
```

```python
import functools

import jax
import jax.numpy as jnp
import numpy as np
from jax import lax
from jax.experimental import pallas as pl
from jax.experimental.pallas import tpu as pltpu
from jax.sharding import Mesh
from jax.sharding import PartitionSpec as P

Q = 64
LANES = 128
HALF = 64
WIDTH = 256
GROUP = 2
TURN = 65536.0
COSINE = (-0.9999992251396179, 19.738981246948242, -64.92865753173828, 85.27162170410156, -58.79049301147461, 21.07110595703125)
VMEM = pl.BlockSpec(memory_space=pltpu.VMEM)
SMEM = pl.BlockSpec(memory_space=pltpu.SMEM)
ANY = pl.BlockSpec(memory_space=pl.ANY)
HBM = pl.BlockSpec(memory_space=pltpu.HBM)


def iota(shape, dim):
    return lax.broadcasted_iota(jnp.int32, shape, dim)


def params(mib):
    return pltpu.CompilerParams(vmem_limit_bytes=mib * 1024 * 1024)


def cost(microseconds):
    return pl.CostEstimate(
        flops=int(microseconds * 1.0e9), bytes_accessed=int(microseconds * 3.0e6), transcendentals=0
    )


def pack_kernel(turning_hbm, bins_hbm, out_ref, turning_ref, bins_ref, sems):
    entries, fine = turning_ref.shape
    rows = fine // 2
    copies = [
        pltpu.make_async_copy(turning_hbm, turning_ref, sems.at[0]),
        pltpu.make_async_copy(bins_hbm, bins_ref, sems.at[1]),
    ]
    for copy in copies:
        copy.start()
    for copy in copies:
        copy.wait()
    codes = jnp.round(turning_ref[...] * (TURN / (2.0 * np.pi)))
    flipped = codes.T
    pair = jnp.concatenate([flipped[:rows], flipped[rows:]], axis=1)
    out_ref[0:rows, :] = pair.astype(jnp.int32).astype(jnp.int16)
    spare = jnp.zeros((out_ref.shape[0] - rows - bins_ref.shape[0], LANES), jnp.int32)
    out_ref[rows:, :] = jnp.concatenate([bins_ref[...], spare], axis=0).astype(jnp.int16)


def stack_kernel(after_ref, *refs):
    del after_ref
    out_ref = refs[-1]
    size = refs[0].shape[0]
    for k, ref in enumerate(refs[:-1]):
        out_ref[k * size : (k + 1) * size, :] = ref[...]


def encode(block):
    top = jnp.max(jnp.max(jnp.abs(block), axis=0, keepdims=True), axis=1, keepdims=True)
    power = jnp.floor(jnp.log2(jnp.maximum(top, 1e-30)))
    code = jnp.clip(jnp.round(block * jnp.exp2(14.0 - power)), -32767.0, 32767.0)
    code = jnp.where(iota(block.shape, 0) == 60, power, code)
    return code.astype(jnp.int32).astype(jnp.int16)


def decode(code):
    code = code.astype(jnp.int32).astype(jnp.float32)
    scale = jnp.exp2(code[60:61, 0:1] - 14.0)
    return code * scale


def rows_kernel(volts_ref, *rest, first, depth):
    held, raw, sems = rest[-3:]
    parts, spectra, stations = volts_ref.shape[:3]
    width = raw.shape[-1]
    steps = raw.shape[0]
    unroll = 4

    def fetch(step):
        return pltpu.make_async_copy(
            volts_ref.at[:, :, :, :, pl.ds(pl.multiple_of(step * width, width), width)],
            raw.at[step, :, :, pl.ds(0, stations)],
            sems.at[step],
        )

    def start(step, _):
        raw[step, :, :, stations:] = jnp.zeros(
            (parts, spectra, raw.shape[3] - stations, 2, width), jnp.bfloat16
        )
        fetch(step).start()
        return 0

    lax.fori_loop(0, steps, start, 0)

    def flip(group, _):
        for unit in range(unroll):
            fetch(group * unroll + unit).wait()
        for unit in range(unroll):
            step = group * unroll + unit
            for k in range(width // LANES):
                block = raw[step, :, :, :, :, k * LANES : (k + 1) * LANES]
                block = block.reshape(parts * spectra * HALF, LANES)
                for t in range(spectra):
                    both = jnp.concatenate(
                        [
                            block[(part * spectra + t) * HALF : (part * spectra + t + 1) * HALF]
                            for part in range(parts)
                        ],
                        axis=0,
                    )
                    at = (step * width + k * LANES) * depth + first + t
                    held[pl.ds(at, LANES, stride=depth), :] = both.astype(jnp.float32).T
        return 0

    lax.fori_loop(0, steps // unroll, flip, 0)


def prepare_kernel(
    place_ref, entry_ref, after_ref, *rest, columns, started, group, near, far, per, fine
):
    del after_ref
    stacks = rest[: len(columns)]
    rest = rest[len(columns) :]
    if started:
        carry_in, found_in, _ = rest[:3]
        rest = rest[3:]
    carry_ref, found_ref, turns_ref, source_ref = rest
    chip = place_ref[0]
    core = place_ref[1]
    x = place_ref[2]
    q_here = source_ref.shape[0]
    per_bits = per.bit_length() - 1
    near_bits = near.bit_length() - 1
    size = fine // 2 + 16
    blocks = [
        (stack, z * size, (chip ^ (z * near + column)) * 2 + (1 - core if other else core))
        for stack, (column, other) in zip(stacks, columns)
        for z in range(far)
    ]

    stations = entry_ref.shape[2]
    twice = (iota((stations, HALF), 0) == (iota((stations, HALF), 1) >> 1)).astype(jnp.bfloat16)
    entries = jnp.concatenate(
        [
            jnp.dot(
                entry_ref[0, pl.ds((group * GROUP + c) ^ x, 1), :]
                .astype(jnp.float32)
                .astype(jnp.bfloat16),
                twice,
                preferred_element_type=jnp.float32,
            )
            for c in range(GROUP)
        ],
        axis=1,
    ).astype(jnp.int32)
    row = iota((2 * LANES, LANES), 0)
    weight = jnp.where(row < LANES, 2.0**-8, 2.0**-16)
    spread = jnp.concatenate(
        [
            jnp.where(
                ((row & (HALF - 1)) == entries) & (((row >> 6) & 1) == half), weight, 0.0
            ).astype(jnp.bfloat16)
            for half in range(2)
        ],
        axis=1,
    )
    code = jnp.concatenate([stack[at : at + fine // 2, :] for stack, at, _ in blocks], axis=0)
    code = code.astype(jnp.int32).astype(jnp.float32)
    high = jnp.floor(code * (1.0 / 256.0))
    digits = jnp.concatenate([high, code - 256.0 * high], axis=1).astype(jnp.bfloat16)
    turns = jnp.dot(digits, spread, preferred_element_type=jnp.float32)
    for index, (_, _, owner) in enumerate(blocks):
        for half in range(2):
            at = pl.multiple_of((owner * 2 + half) * (fine // 2), fine // 2)
            turns_ref[pl.ds(at, fine // 2), :] = turns[
                index * (fine // 2) : (index + 1) * (fine // 2), half * LANES : (half + 1) * LANES
            ]

    if started:
        carry = carry_in[:, 0:1]
        found = found_in[...]
    else:
        carry = jnp.zeros((q_here, 1), jnp.float32)
        found = jnp.zeros((2 * q_here, LANES), jnp.float32)
    lane = iota((q_here, fine), 1)
    hits = []
    for stack, at, _ in blocks:
        tail = stack[at + fine // 2 : at + size, :].astype(jnp.int32)
        bins = jnp.concatenate([tail[r : r + 1, :] for r in range(fine // LANES)], axis=1)
        bin_owner = bins >> per_bits
        relative = (bin_owner >> 1) ^ chip
        label = ((relative & (near - 1)) * far + (relative >> near_bits)) * per
        label = label + (bins & (per - 1))
        label = jnp.where((bin_owner & 1) == core, label, -1)
        hits.append(jnp.where(iota((q_here, fine), 0) == label, 1.0, 0.0))
    above = (iota((fine, fine), 0) < iota((fine, fine), 1)).astype(jnp.bfloat16)
    every = jnp.concatenate(hits, axis=0).astype(jnp.bfloat16)
    every = jnp.dot(every, above, preferred_element_type=jnp.float32)
    ids, at_rank = [], []
    for index, (hit, (_, _, owner)) in enumerate(zip(hits, blocks)):
        before = every[index * q_here : (index + 1) * q_here]
        rank = jnp.sum(hit * (before + carry), axis=0, keepdims=True)
        carry = carry + before[:, fine - 1 : fine] + hit[:, fine - 1 : fine]
        at_rank.append((iota((LANES, fine), 0) == rank.astype(jnp.int32)).astype(jnp.bfloat16))
        high = hit * (owner * (fine // LANES) + (lane >> 7)).astype(jnp.float32)
        low = hit * (lane & (LANES - 1)).astype(jnp.float32)
        ids.append(jnp.concatenate([high, low], axis=0).astype(jnp.bfloat16))
    found = found + lax.dot_general(
        jnp.concatenate(ids, axis=1),
        jnp.concatenate(at_rank, axis=1),
        (((1,), (1,)), ((), ())),
        preferred_element_type=jnp.float32,
    )
    carry_ref[...] = jnp.broadcast_to(carry, carry_ref.shape)
    found_ref[...] = found
    source_ref[...] = (found[:q_here] * LANES + found[q_here:]).astype(jnp.int32)


def wave(z):
    value = jnp.full_like(z, COSINE[-1])
    for coefficient in COSINE[-2::-1]:
        value = value * z + coefficient
    return value


def correlate_kernel(source_ref, held, turns_ref, *rest, first_pair, pairs, spectra):
    outs = rest[:GROUP]
    even, odd, even_turns, odd_turns, wide_even, wide_odd, kept = rest[GROUP:]
    depth = 2 * spectra

    def gather(unit, into, into_turns):
        for first in range(0, LANES, 32):
            at = [source_ref[unit, first + k] for k in range(32)]
            rows = [held[pl.ds(pl.multiple_of(a * depth, depth), depth), :] for a in at]
            turns = [turns_ref[pl.ds(a, 1), :] for a in at]
            for k in range(32):
                into[(first + k) * depth : (first + k + 1) * depth, :] = rows[k]
                into_turns[first + k : first + k + 1, :] = turns[k]

    upper = (iota((HALF, LANES), 1) & (HALF - 1)) > iota((HALF, LANES), 0)
    left = iota((HALF, LANES), 1) < HALF

    def rotate(rows, turns, wide):
        turns = turns[...].T
        turning = []
        for centre in range(GROUP):
            angle = turns[centre * HALF : (centre + 1) * HALF]
            cosine = jnp.abs(angle) - 0.5
            sine = jnp.abs(angle - 0.25) - 0.5
            turning.append((wave(cosine * cosine), wave(sine * sine)))
        for t in range(2 * spectra):
            volts = rows[pl.ds(t, LANES, stride=depth), :].T
            real, imaginary = volts[:HALF], volts[HALF:]
            columns = slice(t * LANES, (t + 1) * LANES)
            for centre in range(GROUP):
                cosine, sine = turning[centre]
                rotated = (real * cosine + imaginary * sine, imaginary * cosine - real * sine)
                for part, value in enumerate(rotated):
                    coarse = value.astype(jnp.bfloat16)
                    rest_of = (value - coarse.astype(jnp.float32)).astype(jnp.bfloat16)
                    wide[centre, part * HALF : (part + 1) * HALF, columns] = coarse
                    wide[centre, LANES + part * HALF : LANES + (part + 1) * HALF, columns] = rest_of

    def correlate(wide):
        results = []
        for centre in range(GROUP):
            product = lax.dot_general(
                wide[centre],
                wide[centre, :LANES],
                (((1,), (1,)), ((), ())),
                preferred_element_type=jnp.float32,
            )
            product = product[:LANES] + product[LANES:]
            under = pltpu.roll(product[HALF:], HALF, 1)
            results.append(product[:HALF] + jnp.where(left, under, -under))
        return results

    def emit(pair, seconds):
        for centre in range(GROUP):
            first, second = kept[centre], seconds[centre]
            first = jnp.where(upper, first, pltpu.roll(first, HALF, 1))
            second = jnp.where(upper, pltpu.roll(second, HALF, 1), second)
            value = jnp.where(left, first, second)
            out_ref = outs[centre]
            if out_ref.dtype == jnp.int16:
                value = encode(value)
            out_ref[pl.ds(pl.multiple_of(pair * HALF, HALF), HALF), :] = value

    base = 2 * first_pair
    last = base + 2 * pairs - 1
    gather(base, even, even_turns)
    wide_odd[...] = jnp.zeros_like(wide_odd)
    kept[...] = jnp.zeros_like(kept)

    def one(pair, _):
        unit = base + 2 * pair
        gather(unit + 1, odd, odd_turns)
        rotate(even, even_turns, wide_even)
        emit(jnp.maximum(pair - 1, 0), correlate(wide_odd))
        gather(jnp.minimum(unit + 2, last), even, even_turns)
        rotate(odd, odd_turns, wide_odd)
        for centre, value in enumerate(correlate(wide_even)):
            kept[centre] = value
        return 0

    lax.fori_loop(0, pairs, one, 0)
    emit(pairs - 1, correlate(wide_odd))


def merge_kernel(own_ref, *refs, arrivals, far, pairs):
    own_out = refs[arrivals]
    outs = refs[arrivals + 1 :]
    for z in range(far):
        for pair in range(pairs):
            at = pl.ds((z * pairs + pair) * HALF, HALF)
            total = own_ref[at, :]
            for ref in refs[:arrivals]:
                total = total + decode(ref[at, :])
            to = pl.ds(pair * HALF, HALF)
            if z == 0:
                own_out[to, :] = total
            else:
                outs[z - 1][to, :] = encode(total)


def finish_kernel(members_ref, own_ref, *refs, arrivals, pairs, scale):
    out_ref = refs[arrivals]
    baselines = members_ref.shape[1]
    first = members_ref[0:1, :]
    second = members_ref[1:2, :]
    rising = first < second
    station = iota((HALF, baselines), 0)
    for pair in range(pairs):
        at = pl.ds(pair * HALF, HALF)
        total = own_ref[at, :]
        for ref in refs[:arrivals]:
            total = total + decode(ref[at, :])
        total = total * scale
        total = jnp.where(iota(total.shape, 0) < 60, total, 0.0)
        flipped = total.T
        coarse = flipped.astype(jnp.bfloat16)
        medium = (flipped - coarse.astype(jnp.float32)).astype(jnp.bfloat16)
        fine = (flipped - coarse.astype(jnp.float32) - medium.astype(jnp.float32)).astype(jnp.bfloat16)
        stack = jnp.concatenate([coarse, medium, fine], axis=0)
        picked = {}
        for side, members in enumerate((first, second)):
            for p in range(2):
                choose = (station == 2 * members + p).astype(jnp.bfloat16)
                rows = jnp.dot(stack, choose, preferred_element_type=jnp.float32)
                rows = rows[:LANES] + rows[LANES : 2 * LANES] + rows[2 * LANES :]
                partner = second if side == 0 else first
                for half in range(2):
                    for p2 in range(2):
                        match = station == 2 * partner + p2
                        part = rows[half * HALF : (half + 1) * HALF]
                        picked[side, half, p, p2] = jnp.sum(
                            jnp.where(match, part, 0.0), axis=0, keepdims=True
                        )
        for half in range(2):
            real, imaginary = [], []
            for p in range(2):
                for p2 in range(2):
                    a = picked[0, half, p, p2]
                    b = picked[1, half, p2, p]
                    real.append(jnp.where(rising, a, b))
                    imaginary.append(jnp.where(rising, b, -a))
            out_ref[2 * pair + half, 0] = jnp.concatenate(real, axis=0)
            out_ref[2 * pair + half, 1] = jnp.concatenate(imaginary, axis=0)


def on_device(volts, entry, turning, members, target, *, tm, chips):
    near = max(1, chips // 4)
    far = chips // near
    fine = turning.shape[1]
    spectra = volts.shape[1]
    centres = entry.shape[1]
    per_device = Q // (2 * chips)
    pairs = per_device // 2
    channels = volts.shape[4]

    def across_chips(x, step):
        return lax.ppermute(x, "chip", [(i, i ^ step) for i in range(chips)])

    def across_cores(x):
        return lax.ppermute(x, "core", [(0, 1), (1, 0)])

    chip = lax.axis_index("chip")
    core = lax.axis_index("core")
    x = lax.axis_index("tm")
    place = jnp.stack([chip, core, x]).astype(jnp.int32)
    other = across_cores(volts)
    block = pl.pallas_call(
        pack_kernel,
        in_specs=[HBM, HBM],
        out_specs=VMEM,
        out_shape=jax.ShapeDtypeStruct((fine // 2 + 16, LANES), jnp.int16),
        scratch_shapes=[
            pltpu.VMEM(turning.shape, jnp.float32),
            pltpu.VMEM((fine // LANES, LANES), jnp.int32),
            pltpu.SemaphoreType.DMA((2,)),
        ],
        compiler_params=params(56),
        cost_estimate=cost(1),
        name="pack",
    )(turning, target.reshape(fine // LANES, LANES))
    line = [block] + [across_chips(block, z * near) for z in range(1, far)]

    held_type = pltpu.VMEM((channels * 2 * spectra, LANES), jnp.float32)

    def rows(side, *operands):
        return pl.pallas_call(
            functools.partial(rows_kernel, first=side * spectra, depth=2 * spectra),
            in_specs=[HBM, ANY, VMEM][: 2 + side],
            out_specs=VMEM,
            out_shape=held_type,
            scratch_shapes=[
                pltpu.VMEM((channels // WIDTH, 2, spectra, 32, 2, WIDTH), jnp.bfloat16),
                pltpu.SemaphoreType.DMA((channels // WIDTH,)),
            ],
            input_output_aliases={2: 0} if side else {},
            compiler_params=params(44),
            cost_estimate=cost(5),
            name="rows",
        )(*operands)

    held = rows(0, volts, place)
    size = block.shape[0]
    stack = pl.pallas_call(
        stack_kernel,
        in_specs=[ANY] + [VMEM] * far,
        out_specs=VMEM,
        out_shape=jax.ShapeDtypeStruct((far * size, LANES), jnp.int16),
        compiler_params=params(4),
        cost_estimate=cost(1),
        name="stack",
    )(held, *line)
    mine = [stack] + [across_chips(stack, y) for y in range(1, near)]
    theirs = [across_cores(stack)]
    held = rows(1, other, place, held)
    each = far * pairs
    arrived = []
    flat = [(a, b) for a in range(tm) for b in range(chips)]

    def exchange(value, c, y):
        route = [(a * chips + b, (a ^ c) * chips + (b ^ y)) for a, b in flat]
        return lax.ppermute(value, ("tm", "chip"), route)

    for group in range(centres // GROUP):
        state = ()
        for part in range(3 if near > 1 else 1):
            if part == 0:
                columns = [(0, False), (0, True)]
            else:
                columns = [(y, part == 2) for y in range(1, near)]
            if part == 1 and group == 0:
                state, mine = lax.optimization_barrier((state, mine))
                theirs += [across_cores(value) for value in mine[1:]]
            stacks = [(theirs if across else mine)[y] for y, across in columns]
            *state, source = pl.pallas_call(
                functools.partial(
                    prepare_kernel,
                    columns=columns,
                    started=part > 0,
                    group=group,
                    near=near,
                    far=far,
                    per=per_device,
                    fine=fine,
                ),
                in_specs=[SMEM, VMEM, ANY] + [VMEM] * (len(stacks) + len(state)),
                out_specs=[VMEM] * 4,
                out_shape=[
                    jax.ShapeDtypeStruct((Q // 2, LANES), jnp.float32),
                    jax.ShapeDtypeStruct((Q, LANES), jnp.float32),
                    pltpu.VMEM((channels, LANES), jnp.float32),
                    jax.ShapeDtypeStruct((Q // 2, LANES), jnp.int32),
                ],
                input_output_aliases={3 + len(stacks) + 2: 2} if part else {},
                compiler_params=params(16),
                cost_estimate=cost(2),
                name="prepare",
            )(place, entry, held, *stacks, *state)
        turns = state[2]
        for y, count in ((1, near - 1), (0, 1)):
            if not count:
                continue
            kinds = [jnp.float32 if group + c + y == 0 else jnp.int16 for c in range(GROUP)]
            results = pl.pallas_call(
                functools.partial(
                    correlate_kernel, first_pair=y * each, pairs=count * each, spectra=spectra
                ),
                in_specs=[SMEM, VMEM, VMEM],
                out_specs=[VMEM] * GROUP,
                out_shape=[
                    jax.ShapeDtypeStruct((count * each * HALF, LANES), kind) for kind in kinds
                ],
                scratch_shapes=[
                    pltpu.VMEM((LANES * 2 * spectra, LANES), jnp.float32),
                    pltpu.VMEM((LANES * 2 * spectra, LANES), jnp.float32),
                    pltpu.VMEM((LANES, LANES), jnp.float32),
                    pltpu.VMEM((LANES, LANES), jnp.float32),
                    pltpu.VMEM((GROUP, 2 * LANES, 2 * spectra * LANES), jnp.bfloat16),
                    pltpu.VMEM((GROUP, 2 * LANES, 2 * spectra * LANES), jnp.bfloat16),
                    pltpu.VMEM((GROUP, HALF, LANES), jnp.float32),
                ],
                compiler_params=params(12),
                cost_estimate=cost(9 * count),
                name="correlate",
            )(source, held, turns)
            for c in range(GROUP):
                for k in range(count):
                    value = results[c]
                    if count > 1:
                        value = value[k * each * HALF : (k + 1) * each * HALF]
                    if group + c + y == 0:
                        total = value
                    else:
                        arrived.append(exchange(value, group * GROUP + c, y + k))
    rows = pairs * HALF
    merged = pl.pallas_call(
        functools.partial(merge_kernel, arrivals=len(arrived), far=far, pairs=pairs),
        in_specs=[VMEM] * (1 + len(arrived)),
        out_specs=[VMEM] * far,
        out_shape=[
            jax.ShapeDtypeStruct((rows, LANES), jnp.int16 if z else jnp.float32)
            for z in range(far)
        ],
        compiler_params=params(6),
        cost_estimate=cost(1),
        name="merge",
    )(total, *arrived)
    final = [across_chips(merged[z], z * near) for z in range(1, far)]
    return pl.pallas_call(
        functools.partial(finish_kernel, arrivals=len(final), pairs=pairs, scale=Q / channels),
        in_specs=[VMEM] * (2 + len(final)),
        out_specs=VMEM,
        out_shape=jax.ShapeDtypeStruct((per_device, 2, 4, members.shape[0]), jnp.float32),
        compiler_params=params(6),
        cost_estimate=cost(2),
        name="finish",
    )(members.T, merged[0], *final)


def solution(mesh):
    tm = mesh.shape["tm"]
    chips = mesh.shape["chan"] // 2
    inner = Mesh(mesh.devices.reshape(tm, chips, 2), ("tm", "chip", "core"))
    every = ("tm", "chip", "core")
    split = ("chip", "core")
    return jax.shard_map(
        functools.partial(on_device, tm=tm, chips=chips),
        mesh=inner,
        in_specs=(
            P(None, every, None, None, None),
            P("tm", None, None),
            P(None, split),
            P(),
            P(split),
        ),
        out_specs=P(every, None, None, None),
        check_vma=False,
    )
```

```python
import functools

import jax
import jax.numpy as jnp
import numpy as np
from jax import lax
from jax.experimental import pallas as pl
from jax.experimental.pallas import tpu as pltpu
from jax.sharding import Mesh
from jax.sharding import PartitionSpec as P

Q = 64
LANES = 128
HALF = 64
WIDTH = 1024
ROW = 8
GROUP = 2
TURN = 65536.0
COSINE = (-0.9999992251396179, 19.738981246948242, -64.92865753173828, 85.27162170410156, -58.79049301147461, 21.07110595703125)
VMEM = pl.BlockSpec(memory_space=pltpu.VMEM)
SMEM = pl.BlockSpec(memory_space=pltpu.SMEM)
ANY = pl.BlockSpec(memory_space=pl.ANY)
HBM = pl.BlockSpec(memory_space=pltpu.HBM)


def iota(shape, dim):
    return lax.broadcasted_iota(jnp.int32, shape, dim)


def params(mib):
    return pltpu.CompilerParams(vmem_limit_bytes=mib * 1024 * 1024)


def cost(microseconds):
    return pl.CostEstimate(
        flops=int(microseconds * 1.0e9), bytes_accessed=int(microseconds * 3.0e6), transcendentals=0
    )


def pack_kernel(turning_hbm, bins_hbm, out_ref, turning_ref, bins_ref, sems):
    entries, fine = turning_ref.shape
    rows = fine // 2
    copies = [
        pltpu.make_async_copy(turning_hbm, turning_ref, sems.at[0]),
        pltpu.make_async_copy(bins_hbm, bins_ref, sems.at[1]),
    ]
    for copy in copies:
        copy.start()
    for copy in copies:
        copy.wait()
    codes = jnp.round(turning_ref[...] * (TURN / (2.0 * np.pi)))
    flipped = codes.T
    pair = jnp.concatenate([flipped[:rows], flipped[rows:]], axis=1)
    out_ref[0:rows, :] = pair.astype(jnp.int32).astype(jnp.int16)
    spare = jnp.zeros((out_ref.shape[0] - rows - bins_ref.shape[0], LANES), jnp.int32)
    out_ref[rows:, :] = jnp.concatenate([bins_ref[...], spare], axis=0).astype(jnp.int16)


def stack_kernel(after_ref, *refs):
    del after_ref
    out_ref = refs[-1]
    size = refs[0].shape[0]
    for k, ref in enumerate(refs[:-1]):
        out_ref[k * size : (k + 1) * size, :] = ref[...]


def encode(block):
    top = jnp.max(jnp.max(jnp.abs(block), axis=0, keepdims=True), axis=1, keepdims=True)
    power = jnp.floor(jnp.log2(jnp.maximum(top, 1e-30)))
    code = jnp.clip(jnp.round(block * jnp.exp2(14.0 - power)), -32767.0, 32767.0)
    code = jnp.where(iota(block.shape, 0) == 60, power, code)
    return code.astype(jnp.int32).astype(jnp.int16)


def decode(code):
    code = code.astype(jnp.int32).astype(jnp.float32)
    scale = jnp.exp2(code[60:61, 0:1] - 14.0)
    return code * scale


def rows_kernel(volts_ref, *rest, first, pitch):
    held, raw, sems = rest[-3:]
    parts, spectra, stations = volts_ref.shape[:3]
    width = raw.shape[-1]
    steps = raw.shape[0]
    unroll = 2

    def fetch(step):
        return pltpu.make_async_copy(
            volts_ref.at[:, :, :, :, pl.ds(pl.multiple_of(step * width, width), width)],
            raw.at[step, :, :, pl.ds(0, stations)],
            sems.at[step],
        )

    def start(step, _):
        raw[step, :, :, stations:] = jnp.zeros(
            (parts, spectra, raw.shape[3] - stations, 2, width), jnp.bfloat16
        )
        fetch(step).start()
        return 0

    lax.fori_loop(0, steps, start, 0)

    def flip(group, _):
        for unit in range(unroll):
            fetch(group * unroll + unit).wait()
        for unit in range(unroll):
            step = group * unroll + unit
            for k in range(width // LANES):
                block = raw[step, :, :, :, :, k * LANES : (k + 1) * LANES]
                block = block.reshape(parts * spectra * HALF, LANES)
                for t in range(spectra):
                    both = jnp.concatenate(
                        [
                            block[(part * spectra + t) * HALF : (part * spectra + t + 1) * HALF]
                            for part in range(parts)
                        ],
                        axis=0,
                    )
                    at = (step * width + k * LANES) * pitch + first + t
                    held[pl.ds(at, LANES, stride=pitch), :] = both.astype(jnp.float32).T
        return 0

    lax.fori_loop(0, steps // unroll, flip, 0)


def prepare_kernel(
    place_ref, entry_ref, after_ref, held_in, *rest, columns, started, group, near, far, per, fine, pitch
):
    del after_ref, held_in
    stacks = rest[: len(columns)]
    rest = rest[len(columns) :]
    if started:
        carry_in, found_in = rest[:2]
        rest = rest[2:]
    held, carry_ref, found_ref, source_ref = rest
    chip = place_ref[0]
    core = place_ref[1]
    x = place_ref[2]
    q_here = source_ref.shape[0]
    per_bits = per.bit_length() - 1
    near_bits = near.bit_length() - 1
    size = fine // 2 + 16
    blocks = [
        (stack, z * size, (chip ^ (z * near + column)) * 2 + (1 - core if other else core))
        for stack, (column, other) in zip(stacks, columns)
        for z in range(far)
    ]

    stations = entry_ref.shape[2]
    twice = (iota((stations, HALF), 0) == (iota((stations, HALF), 1) >> 1)).astype(jnp.bfloat16)
    entries = jnp.concatenate(
        [
            jnp.dot(
                entry_ref[0, pl.ds((group * GROUP + c) ^ x, 1), :]
                .astype(jnp.float32)
                .astype(jnp.bfloat16),
                twice,
                preferred_element_type=jnp.float32,
            )
            for c in range(GROUP)
        ],
        axis=1,
    ).astype(jnp.int32)
    row = iota((2 * LANES, LANES), 0)
    weight = jnp.where(row < LANES, 2.0**-8, 2.0**-16)
    spread = jnp.concatenate(
        [
            jnp.where(
                ((row & (HALF - 1)) == entries) & (((row >> 6) & 1) == half), weight, 0.0
            ).astype(jnp.bfloat16)
            for half in range(2)
        ],
        axis=1,
    )
    code = jnp.concatenate([stack[at : at + fine // 2, :] for stack, at, _ in blocks], axis=0)
    code = code.astype(jnp.int32).astype(jnp.float32)
    high = jnp.floor(code * (1.0 / 256.0))
    digits = jnp.concatenate([high, code - 256.0 * high], axis=1).astype(jnp.bfloat16)
    turns = jnp.dot(digits, spread, preferred_element_type=jnp.float32)
    for index, (_, _, owner) in enumerate(blocks):
        for half in range(2):
            at = (owner * 2 + half) * (fine // 2) * pitch + pitch - 1
            held[pl.ds(at, fine // 2, stride=pitch), :] = turns[
                index * (fine // 2) : (index + 1) * (fine // 2), half * LANES : (half + 1) * LANES
            ]

    if started:
        carry = carry_in[:, 0:1]
        found = found_in[...]
    else:
        carry = jnp.zeros((q_here, 1), jnp.float32)
        found = jnp.zeros((2 * q_here, LANES), jnp.float32)
    lane = iota((q_here, fine), 1)
    hits = []
    for stack, at, _ in blocks:
        tail = stack[at + fine // 2 : at + size, :].astype(jnp.int32)
        bins = jnp.concatenate([tail[r : r + 1, :] for r in range(fine // LANES)], axis=1)
        bin_owner = bins >> per_bits
        relative = (bin_owner >> 1) ^ chip
        label = ((relative & (near - 1)) * far + (relative >> near_bits)) * per
        label = label + (bins & (per - 1))
        label = jnp.where((bin_owner & 1) == core, label, -1)
        hits.append(jnp.where(iota((q_here, fine), 0) == label, 1.0, 0.0))
    above = (iota((fine, fine), 0) < iota((fine, fine), 1)).astype(jnp.bfloat16)
    every = jnp.concatenate(hits, axis=0).astype(jnp.bfloat16)
    every = jnp.dot(every, above, preferred_element_type=jnp.float32)
    ids, at_rank = [], []
    for index, (hit, (_, _, owner)) in enumerate(zip(hits, blocks)):
        before = every[index * q_here : (index + 1) * q_here]
        rank = jnp.sum(hit * (before + carry), axis=0, keepdims=True)
        carry = carry + before[:, fine - 1 : fine] + hit[:, fine - 1 : fine]
        at_rank.append((iota((LANES, fine), 0) == rank.astype(jnp.int32)).astype(jnp.bfloat16))
        high = hit * (owner * (fine // LANES) + (lane >> 7)).astype(jnp.float32)
        low = hit * (lane & (LANES - 1)).astype(jnp.float32)
        ids.append(jnp.concatenate([high, low], axis=0).astype(jnp.bfloat16))
    found = found + lax.dot_general(
        jnp.concatenate(ids, axis=1),
        jnp.concatenate(at_rank, axis=1),
        (((1,), (1,)), ((), ())),
        preferred_element_type=jnp.float32,
    )
    carry_ref[...] = jnp.broadcast_to(carry, carry_ref.shape)
    found_ref[...] = found
    source_ref[...] = ((found[:q_here] * LANES + found[q_here:]) * pitch).astype(jnp.int32)


def wave(z):
    value = jnp.full_like(z, COSINE[-1])
    for coefficient in COSINE[-2::-1]:
        value = value * z + coefficient
    return value


def correlate_kernel(source_ref, held, *rest, first_pair, pairs, spectra, sent):
    outs = rest[: 1 if sent else GROUP]
    rest = rest[len(outs) :]
    even, odd, wide_even, wide_odd, kept = rest

    def gather(unit, into):
        for first in range(0, LANES, 32):
            at = [source_ref[unit, first + k] for k in range(32)]
            rows = [held[pl.ds(a, ROW), :] for a in at]
            for k in range(32):
                into[(first + k) * ROW : (first + k + 1) * ROW, :] = rows[k]

    upper = (iota((HALF, LANES), 1) & (HALF - 1)) > iota((HALF, LANES), 0)
    left = iota((HALF, LANES), 1) < HALF

    def rotate(rows, wide):
        turns = rows[pl.ds(2 * spectra, LANES, stride=ROW), :].T
        turning = []
        for centre in range(GROUP):
            angle = turns[centre * HALF : (centre + 1) * HALF]
            cosine = jnp.abs(angle) - 0.5
            sine = jnp.abs(angle - 0.25) - 0.5
            turning.append((wave(cosine * cosine), wave(sine * sine)))
        for t in range(2 * spectra):
            volts = rows[pl.ds(t, LANES, stride=ROW), :].T
            real, imaginary = volts[:HALF], volts[HALF:]
            columns = slice(t * LANES, (t + 1) * LANES)
            for centre in range(GROUP):
                cosine, sine = turning[centre]
                rotated = (real * cosine + imaginary * sine, imaginary * cosine - real * sine)
                for part, value in enumerate(rotated):
                    coarse = value.astype(jnp.bfloat16)
                    rest_of = (value - coarse.astype(jnp.float32)).astype(jnp.bfloat16)
                    wide[centre, part * HALF : (part + 1) * HALF, columns] = coarse
                    wide[centre, LANES + part * HALF : LANES + (part + 1) * HALF, columns] = rest_of

    def correlate(wide):
        results = []
        for centre in range(GROUP):
            product = lax.dot_general(
                wide[centre],
                wide[centre, :LANES],
                (((1,), (1,)), ((), ())),
                preferred_element_type=jnp.float32,
            )
            product = product[:LANES] + product[LANES:]
            under = pltpu.roll(product[HALF:], HALF, 1)
            results.append(product[:HALF] + jnp.where(left, under, -under))
        return results

    def emit(pair, seconds):
        for centre in range(GROUP):
            first, second = kept[centre], seconds[centre]
            first = jnp.where(upper, first, pltpu.roll(first, HALF, 1))
            second = jnp.where(upper, pltpu.roll(second, HALF, 1), second)
            value = jnp.where(left, first, second)
            at = pl.ds(pl.multiple_of(pair * HALF, HALF), HALF)
            if outs[0].dtype == jnp.int16:
                value = encode(value)
                outs[0][centre, at, :] = value
            else:
                outs[centre][at, :] = value

    base = 2 * first_pair
    last = base + 2 * pairs - 1
    gather(base, even)
    wide_odd[...] = jnp.zeros_like(wide_odd)
    kept[...] = jnp.zeros_like(kept)

    def one(pair, _):
        unit = base + 2 * pair
        gather(unit + 1, odd)
        rotate(even, wide_even)
        emit(jnp.maximum(pair - 1, 0), correlate(wide_odd))
        gather(jnp.minimum(unit + 2, last), even)
        rotate(odd, wide_odd)
        for centre, value in enumerate(correlate(wide_even)):
            kept[centre] = value
        return 0

    lax.fori_loop(0, pairs, one, 0)
    emit(pairs - 1, correlate(wide_odd))


def join_kernel(*refs, arrivals):
    owns, arrived, outs = refs[:GROUP], refs[GROUP : GROUP + arrivals], refs[GROUP + arrivals :]
    for at in range(0, owns[0].shape[0], HALF):
        for c in range(GROUP):
            value = owns[c][at : at + HALF, :]
            for ref in arrived:
                value = value + decode(ref[c, at : at + HALF, :])
            outs[c][at : at + HALF, :] = encode(value) if outs[c].dtype == jnp.int16 else value


def merge_kernel(own_ref, *refs, arrivals, far, pairs):
    own_out = refs[arrivals]
    outs = refs[arrivals + 1 :]
    for z in range(far):
        for pair in range(pairs):
            at = pl.ds((z * pairs + pair) * HALF, HALF)
            total = own_ref[at, :]
            for ref in refs[:arrivals]:
                total = total + decode(ref[at, :])
            to = pl.ds(pair * HALF, HALF)
            if z == 0:
                own_out[to, :] = total
            else:
                outs[z - 1][to, :] = encode(total)


def finish_kernel(members_ref, own_ref, *refs, arrivals, pairs, scale):
    out_ref = refs[arrivals]
    baselines = members_ref.shape[1]
    first = members_ref[0:1, :]
    second = members_ref[1:2, :]
    rising = first < second
    station = iota((HALF, baselines), 0)
    for pair in range(pairs):
        at = pl.ds(pair * HALF, HALF)
        total = own_ref[at, :]
        for ref in refs[:arrivals]:
            total = total + decode(ref[at, :])
        total = total * scale
        total = jnp.where(iota(total.shape, 0) < 60, total, 0.0)
        flipped = total.T
        coarse = flipped.astype(jnp.bfloat16)
        medium = (flipped - coarse.astype(jnp.float32)).astype(jnp.bfloat16)
        stack = jnp.concatenate([coarse, medium], axis=0)
        picked = {}
        for side, members in enumerate((first, second)):
            for p in range(2):
                choose = (station == 2 * members + p).astype(jnp.bfloat16)
                rows = jnp.dot(stack, choose, preferred_element_type=jnp.float32)
                rows = rows[:LANES] + rows[LANES:]
                partner = second if side == 0 else first
                for half in range(2):
                    for p2 in range(2):
                        match = station == 2 * partner + p2
                        part = rows[half * HALF : (half + 1) * HALF]
                        picked[side, half, p, p2] = jnp.sum(
                            jnp.where(match, part, 0.0), axis=0, keepdims=True
                        )
        for half in range(2):
            real, imaginary = [], []
            for p in range(2):
                for p2 in range(2):
                    a = picked[0, half, p, p2]
                    b = picked[1, half, p2, p]
                    real.append(jnp.where(rising, a, b))
                    imaginary.append(jnp.where(rising, b, -a))
            out_ref[2 * pair + half, 0] = jnp.concatenate(real, axis=0)
            out_ref[2 * pair + half, 1] = jnp.concatenate(imaginary, axis=0)


def on_device(volts, entry, turning, members, target, *, tm, chips):
    near = max(1, chips // 4)
    far = chips // near
    fine = turning.shape[1]
    spectra = volts.shape[1]
    centres = entry.shape[1]
    per_device = Q // (2 * chips)
    pairs = per_device // 2
    channels = volts.shape[4]

    def across_chips(x, step):
        return lax.ppermute(x, "chip", [(i, i ^ step) for i in range(chips)])

    def across_cores(x):
        return lax.ppermute(x, "core", [(0, 1), (1, 0)])

    chip = lax.axis_index("chip")
    core = lax.axis_index("core")
    x = lax.axis_index("tm")
    place = jnp.stack([chip, core, x]).astype(jnp.int32)
    other = across_cores(volts)
    block = pl.pallas_call(
        pack_kernel,
        in_specs=[HBM, HBM],
        out_specs=VMEM,
        out_shape=jax.ShapeDtypeStruct((fine // 2 + 16, LANES), jnp.int16),
        scratch_shapes=[
            pltpu.VMEM(turning.shape, jnp.float32),
            pltpu.VMEM((fine // LANES, LANES), jnp.int32),
            pltpu.SemaphoreType.DMA((2,)),
        ],
        compiler_params=params(56),
        cost_estimate=cost(1),
        name="pack",
    )(turning, target.reshape(fine // LANES, LANES))
    line = [block] + [across_chips(block, z * near) for z in range(1, far)]

    pitch = 2 * spectra + 1
    held_type = pltpu.VMEM((channels * pitch + ROW, LANES), jnp.float32)

    def rows(side, *operands):
        return pl.pallas_call(
            functools.partial(rows_kernel, first=side * spectra, pitch=pitch),
            in_specs=[HBM, ANY, VMEM][: 2 + side],
            out_specs=VMEM,
            out_shape=held_type,
            scratch_shapes=[
                pltpu.VMEM((channels // WIDTH, 2, spectra, 32, 2, WIDTH), jnp.bfloat16),
                pltpu.SemaphoreType.DMA((channels // WIDTH,)),
            ],
            input_output_aliases={2: 0} if side else {},
            compiler_params=params(40),
            cost_estimate=cost(5),
            name="rows",
        )(*operands)

    held = rows(0, volts, place)
    size = block.shape[0]
    stack = pl.pallas_call(
        stack_kernel,
        in_specs=[ANY] + [VMEM] * far,
        out_specs=VMEM,
        out_shape=jax.ShapeDtypeStruct((far * size, LANES), jnp.int16),
        compiler_params=params(4),
        cost_estimate=cost(1),
        name="stack",
    )(held, *line)
    mine = [stack] + [across_chips(stack, y) for y in range(1, near)]
    theirs = [across_cores(stack)]
    held = rows(1, other, place, held)
    each = far * pairs
    arrived = []
    after = place
    for group in range(centres // GROUP):
        state = ()
        for part in range(3 if near > 1 else 1):
            if part == 0:
                columns = [(0, False), (0, True)]
            else:
                columns = [(y, part == 2) for y in range(1, near)]
            if part == 1 and group == 0:
                state, mine = lax.optimization_barrier((state, mine))
                theirs += [across_cores(value) for value in mine[1:]]
            stacks = [(theirs if across else mine)[y] for y, across in columns]
            held, *state, source = pl.pallas_call(
                functools.partial(
                    prepare_kernel,
                    columns=columns,
                    started=part > 0,
                    group=group,
                    near=near,
                    far=far,
                    per=per_device,
                    fine=fine,
                    pitch=pitch,
                ),
                in_specs=[SMEM, VMEM, ANY] + [VMEM] * (1 + len(stacks) + len(state)),
                out_specs=[VMEM] * 4,
                out_shape=[
                    held_type,
                    jax.ShapeDtypeStruct((Q // 2, LANES), jnp.float32),
                    jax.ShapeDtypeStruct((Q, LANES), jnp.float32),
                    jax.ShapeDtypeStruct((Q // 2, LANES), jnp.int32),
                ],
                input_output_aliases={3: 0},
                compiler_params=params(16),
                cost_estimate=cost(2),
                name="prepare",
            )(place, entry, after, held, *stacks, *state)
        def correlate(first_pair, out_types, source=source, held=held):
            return pl.pallas_call(
                functools.partial(
                    correlate_kernel,
                    first_pair=first_pair,
                    pairs=each,
                    spectra=spectra,
                    sent=len(out_types) == 1,
                ),
                in_specs=[SMEM, VMEM],
                out_specs=[VMEM] * len(out_types),
                out_shape=out_types,
                scratch_shapes=[
                    pltpu.VMEM((LANES * ROW, LANES), jnp.float32),
                    pltpu.VMEM((LANES * ROW, LANES), jnp.float32),
                    pltpu.VMEM((GROUP, 2 * LANES, 2 * spectra * LANES), jnp.bfloat16),
                    pltpu.VMEM((GROUP, 2 * LANES, 2 * spectra * LANES), jnp.bfloat16),
                    pltpu.VMEM((GROUP, HALF, LANES), jnp.float32),
                ],
                compiler_params=params(12),
                cost_estimate=cost(9),
                name="correlate",
            )(source, held)

        columns_in = []
        for y in range(1, near):
            sent = correlate(
                y * each, [jax.ShapeDtypeStruct((GROUP, each * HALF, LANES), jnp.int16)]
            )[0]
            columns_in.append(across_chips(sent, y))
        own = correlate(0, [jax.ShapeDtypeStruct((each * HALF, LANES), jnp.float32)] * GROUP)
        after = own[0]
        if columns_in:
            kinds = [jnp.int16 if group + c else jnp.float32 for c in range(GROUP)]
            own = pl.pallas_call(
                functools.partial(join_kernel, arrivals=len(columns_in)),
                in_specs=[VMEM] * (GROUP + len(columns_in)),
                out_specs=[VMEM] * GROUP,
                out_shape=[jax.ShapeDtypeStruct((each * HALF, LANES), kind) for kind in kinds],
                compiler_params=params(8),
                cost_estimate=cost(1),
                name="join",
            )(*own, *columns_in)
        for c in range(GROUP):
            centre = group * GROUP + c
            if centre == 0:
                total = own[c]
            else:
                arrived.append(
                    lax.ppermute(own[c], "tm", [(i, i ^ centre) for i in range(tm)])
                )
    rows = pairs * HALF
    merged = pl.pallas_call(
        functools.partial(merge_kernel, arrivals=len(arrived), far=far, pairs=pairs),
        in_specs=[VMEM] * (1 + len(arrived)),
        out_specs=[VMEM] * far,
        out_shape=[
            jax.ShapeDtypeStruct((rows, LANES), jnp.int16 if z else jnp.float32)
            for z in range(far)
        ],
        compiler_params=params(6),
        cost_estimate=cost(1),
        name="merge",
    )(total, *arrived)
    final = [across_chips(merged[z], z * near) for z in range(1, far)]
    return pl.pallas_call(
        functools.partial(finish_kernel, arrivals=len(final), pairs=pairs, scale=Q / channels),
        in_specs=[VMEM] * (2 + len(final)),
        out_specs=VMEM,
        out_shape=jax.ShapeDtypeStruct((per_device, 2, 4, members.shape[0]), jnp.float32),
        compiler_params=params(6),
        cost_estimate=cost(2),
        name="finish",
    )(members.T, merged[0], *final)


def solution(mesh):
    tm = mesh.shape["tm"]
    chips = mesh.shape["chan"] // 2
    inner = Mesh(mesh.devices.reshape(tm, chips, 2), ("tm", "chip", "core"))
    every = ("tm", "chip", "core")
    split = ("chip", "core")
    return jax.shard_map(
        functools.partial(on_device, tm=tm, chips=chips),
        mesh=inner,
        in_specs=(
            P(None, every, None, None, None),
            P("tm", None, None),
            P(None, split),
            P(),
            P(split),
        ),
        out_specs=P(every, None, None, None),
        check_vma=False,
    )
```

```python
import functools

import jax
import jax.numpy as jnp
import numpy as np
from jax import lax
from jax.experimental import pallas as pl
from jax.experimental.pallas import tpu as pltpu
from jax.sharding import Mesh
from jax.sharding import PartitionSpec as P

Q = 64
LANES = 128
HALF = 64
WIDTH = 1024
ROW = 8
GROUP = 2
TURN = 65536.0
COSINE = (-0.9999992251396179, 19.738981246948242, -64.92865753173828, 85.27162170410156, -58.79049301147461, 21.07110595703125)
VMEM = pl.BlockSpec(memory_space=pltpu.VMEM)
SMEM = pl.BlockSpec(memory_space=pltpu.SMEM)
ANY = pl.BlockSpec(memory_space=pl.ANY)
HBM = pl.BlockSpec(memory_space=pltpu.HBM)


def iota(shape, dim):
    return lax.broadcasted_iota(jnp.int32, shape, dim)


def params(mib):
    return pltpu.CompilerParams(vmem_limit_bytes=mib * 1024 * 1024)


def cost(microseconds):
    return pl.CostEstimate(
        flops=int(microseconds * 1.0e9), bytes_accessed=int(microseconds * 3.0e6), transcendentals=0
    )


def pack_kernel(turning_hbm, bins_hbm, out_ref, turning_ref, bins_ref, sems):
    entries, fine = turning_ref.shape
    rows = fine // 2
    copies = [
        pltpu.make_async_copy(turning_hbm, turning_ref, sems.at[0]),
        pltpu.make_async_copy(bins_hbm, bins_ref, sems.at[1]),
    ]
    for copy in copies:
        copy.start()
    for copy in copies:
        copy.wait()
    codes = jnp.round(turning_ref[...] * (TURN / (2.0 * np.pi)))
    flipped = codes.T
    pair = jnp.concatenate([flipped[:rows], flipped[rows:]], axis=1)
    out_ref[0:rows, :] = pair.astype(jnp.int32).astype(jnp.int16)
    spare = jnp.zeros((out_ref.shape[0] - rows - bins_ref.shape[0], LANES), jnp.int32)
    out_ref[rows:, :] = jnp.concatenate([bins_ref[...], spare], axis=0).astype(jnp.int16)


def stack_kernel(after_ref, *refs):
    del after_ref
    out_ref = refs[-1]
    size = refs[0].shape[0]
    for k, ref in enumerate(refs[:-1]):
        out_ref[k * size : (k + 1) * size, :] = ref[...]


def encode(block):
    top = jnp.max(jnp.max(jnp.abs(block), axis=0, keepdims=True), axis=1, keepdims=True)
    power = jnp.floor(jnp.log2(jnp.maximum(top, 1e-30)))
    code = jnp.clip(jnp.round(block * jnp.exp2(14.0 - power)), -32767.0, 32767.0)
    code = jnp.where(iota(block.shape, 0) == 60, power, code)
    return code.astype(jnp.int32).astype(jnp.int16)


def decode(code):
    code = code.astype(jnp.int32).astype(jnp.float32)
    scale = jnp.exp2(code[60:61, 0:1] - 14.0)
    return code * scale


def rows_kernel(volts_ref, *rest, first, pitch):
    held, raw, sems = rest[-3:]
    parts, spectra, stations = volts_ref.shape[:3]
    width = raw.shape[-1]
    steps = raw.shape[0]
    unroll = 2

    def fetch(step):
        return pltpu.make_async_copy(
            volts_ref.at[:, :, :, :, pl.ds(pl.multiple_of(step * width, width), width)],
            raw.at[step, :, :, pl.ds(0, stations)],
            sems.at[step],
        )

    def start(step, _):
        raw[step, :, :, stations:] = jnp.zeros(
            (parts, spectra, raw.shape[3] - stations, 2, width), jnp.bfloat16
        )
        fetch(step).start()
        return 0

    lax.fori_loop(0, steps, start, 0)

    def flip(group, _):
        for unit in range(unroll):
            fetch(group * unroll + unit).wait()
        for unit in range(unroll):
            step = group * unroll + unit
            for k in range(width // LANES):
                block = raw[step, :, :, :, :, k * LANES : (k + 1) * LANES]
                block = block.reshape(parts * spectra * HALF, LANES)
                for t in range(spectra):
                    both = jnp.concatenate(
                        [
                            block[(part * spectra + t) * HALF : (part * spectra + t + 1) * HALF]
                            for part in range(parts)
                        ],
                        axis=0,
                    )
                    at = (step * width + k * LANES) * pitch + first + t
                    held[pl.ds(at, LANES, stride=pitch), :] = both.astype(jnp.float32).T
        return 0

    lax.fori_loop(0, steps // unroll, flip, 0)


def prepare_kernel(
    chip_ref, core_ref, x_ref, entry_ref, after_ref, held_in, *rest, columns, started, group, near, far, per, fine, pitch
):
    del after_ref, held_in
    stacks = rest[: len(columns)]
    rest = rest[len(columns) :]
    if started:
        carry_in, found_in = rest[:2]
        rest = rest[2:]
    held, carry_ref, found_ref, source_ref = rest
    chip = chip_ref[0]
    core = core_ref[0]
    x = x_ref[0]
    q_here = source_ref.shape[0]
    per_bits = per.bit_length() - 1
    near_bits = near.bit_length() - 1
    size = fine // 2 + 16
    blocks = [
        (stack, z * size, (chip ^ (z * near + column)) * 2 + (1 - core if other else core))
        for stack, (column, other) in zip(stacks, columns)
        for z in range(far)
    ]

    stations = entry_ref.shape[2]
    twice = (iota((stations, HALF), 0) == (iota((stations, HALF), 1) >> 1)).astype(jnp.bfloat16)
    entries = jnp.concatenate(
        [
            jnp.dot(
                entry_ref[0, pl.ds((group * GROUP + c) ^ x, 1), :]
                .astype(jnp.float32)
                .astype(jnp.bfloat16),
                twice,
                preferred_element_type=jnp.float32,
            )
            for c in range(GROUP)
        ],
        axis=1,
    ).astype(jnp.int32)
    row = iota((2 * LANES, LANES), 0)
    weight = jnp.where(row < LANES, 2.0**-8, 2.0**-16)
    spread = jnp.concatenate(
        [
            jnp.where(
                ((row & (HALF - 1)) == entries) & (((row >> 6) & 1) == half), weight, 0.0
            ).astype(jnp.bfloat16)
            for half in range(2)
        ],
        axis=1,
    )
    code = jnp.concatenate([stack[at : at + fine // 2, :] for stack, at, _ in blocks], axis=0)
    code = code.astype(jnp.int32).astype(jnp.float32)
    high = jnp.floor(code * (1.0 / 256.0))
    digits = jnp.concatenate([high, code - 256.0 * high], axis=1).astype(jnp.bfloat16)
    turns = jnp.dot(digits, spread, preferred_element_type=jnp.float32)
    for index, (_, _, owner) in enumerate(blocks):
        for half in range(2):
            at = (owner * 2 + half) * (fine // 2) * pitch + pitch - 1
            held[pl.ds(at, fine // 2, stride=pitch), :] = turns[
                index * (fine // 2) : (index + 1) * (fine // 2), half * LANES : (half + 1) * LANES
            ]

    if started:
        carry = carry_in[:, 0:1]
        found = found_in[...]
    else:
        carry = jnp.zeros((q_here, 1), jnp.float32)
        found = jnp.zeros((2 * q_here, LANES), jnp.float32)
    lane = iota((q_here, fine), 1)
    hits = []
    for stack, at, _ in blocks:
        tail = stack[at + fine // 2 : at + size, :].astype(jnp.int32)
        bins = jnp.concatenate([tail[r : r + 1, :] for r in range(fine // LANES)], axis=1)
        bin_owner = bins >> per_bits
        relative = (bin_owner >> 1) ^ chip
        label = ((relative & (near - 1)) * far + (relative >> near_bits)) * per
        label = label + (bins & (per - 1))
        label = jnp.where((bin_owner & 1) == core, label, -1)
        hits.append(jnp.where(iota((q_here, fine), 0) == label, 1.0, 0.0))
    above = (iota((fine, fine), 0) < iota((fine, fine), 1)).astype(jnp.bfloat16)
    every = jnp.concatenate(hits, axis=0).astype(jnp.bfloat16)
    every = jnp.dot(every, above, preferred_element_type=jnp.float32)
    ids, at_rank = [], []
    for index, (hit, (_, _, owner)) in enumerate(zip(hits, blocks)):
        before = every[index * q_here : (index + 1) * q_here]
        rank = jnp.sum(hit * (before + carry), axis=0, keepdims=True)
        carry = carry + before[:, fine - 1 : fine] + hit[:, fine - 1 : fine]
        at_rank.append((iota((LANES, fine), 0) == rank.astype(jnp.int32)).astype(jnp.bfloat16))
        high = hit * (owner * (fine // LANES) + (lane >> 7)).astype(jnp.float32)
        low = hit * (lane & (LANES - 1)).astype(jnp.float32)
        ids.append(jnp.concatenate([high, low], axis=0).astype(jnp.bfloat16))
    found = found + lax.dot_general(
        jnp.concatenate(ids, axis=1),
        jnp.concatenate(at_rank, axis=1),
        (((1,), (1,)), ((), ())),
        preferred_element_type=jnp.float32,
    )
    carry_ref[...] = jnp.broadcast_to(carry, carry_ref.shape)
    found_ref[...] = found
    source_ref[...] = ((found[:q_here] * LANES + found[q_here:]) * pitch).astype(jnp.int32)


def wave(z):
    value = jnp.full_like(z, COSINE[-1])
    for coefficient in COSINE[-2::-1]:
        value = value * z + coefficient
    return value


def correlate_kernel(source_ref, held, *rest, first_pair, pairs, spectra, sent):
    outs = rest[: 1 if sent else GROUP]
    rest = rest[len(outs) :]
    even, odd, wide_even, wide_odd, kept = rest[:5]
    sums = rest[5:] if sent else outs

    def gather(unit, into):
        for first in range(0, LANES, 32):
            at = [source_ref[unit, first + k] for k in range(32)]
            rows = [held[pl.ds(a, ROW), :] for a in at]
            for k in range(32):
                into[(first + k) * ROW : (first + k + 1) * ROW, :] = rows[k]

    upper = (iota((HALF, LANES), 1) & (HALF - 1)) > iota((HALF, LANES), 0)
    left = iota((HALF, LANES), 1) < HALF

    def rotate(rows, wide):
        turns = rows[pl.ds(2 * spectra, LANES, stride=ROW), :].T
        turning = []
        for centre in range(GROUP):
            angle = turns[centre * HALF : (centre + 1) * HALF]
            cosine = jnp.abs(angle) - 0.5
            sine = jnp.abs(angle - 0.25) - 0.5
            turning.append((wave(cosine * cosine), wave(sine * sine)))
        for t in range(2 * spectra):
            volts = rows[pl.ds(t, LANES, stride=ROW), :].T
            real, imaginary = volts[:HALF], volts[HALF:]
            columns = slice(t * LANES, (t + 1) * LANES)
            for centre in range(GROUP):
                cosine, sine = turning[centre]
                rotated = (real * cosine + imaginary * sine, imaginary * cosine - real * sine)
                for part, value in enumerate(rotated):
                    coarse = value.astype(jnp.bfloat16)
                    rest_of = (value - coarse.astype(jnp.float32)).astype(jnp.bfloat16)
                    wide[centre, part * HALF : (part + 1) * HALF, columns] = coarse
                    wide[centre, LANES + part * HALF : LANES + (part + 1) * HALF, columns] = rest_of

    def correlate(wide):
        results = []
        for centre in range(GROUP):
            product = lax.dot_general(
                wide[centre],
                wide[centre, :LANES],
                (((1,), (1,)), ((), ())),
                preferred_element_type=jnp.float32,
            )
            product = product[:LANES] + product[LANES:]
            under = pltpu.roll(product[HALF:], HALF, 1)
            results.append(product[:HALF] + jnp.where(left, under, -under))
        return results

    def emit(pair, seconds):
        for centre in range(GROUP):
            first, second = kept[centre], seconds[centre]
            first = jnp.where(upper, first, pltpu.roll(first, HALF, 1))
            second = jnp.where(upper, pltpu.roll(second, HALF, 1), second)
            value = jnp.where(left, first, second)
            at = pl.ds(pl.multiple_of(pair * HALF, HALF), HALF)
            sums[centre][at, :] = value

    base = 2 * first_pair
    last = base + 2 * pairs - 1
    gather(base, even)

    def one(pair, _):
        unit = base + 2 * pair
        gather(unit + 1, odd)
        rotate(even, wide_even)
        emit(jnp.maximum(pair - 1, 0), correlate(wide_odd))
        gather(jnp.minimum(unit + 2, last), even)
        rotate(odd, wide_odd)
        for centre, value in enumerate(correlate(wide_even)):
            kept[centre] = value
        return 0

    lax.fori_loop(0, pairs, one, 0)
    emit(pairs - 1, correlate(wide_odd))
    if sent:
        for centre in range(GROUP):
            for pair in range(pairs):
                at = slice(pair * HALF, (pair + 1) * HALF)
                outs[0][centre, at, :] = encode(sums[centre][at, :])


def join_kernel(*refs, arrivals):
    owns, arrived, outs = refs[:GROUP], refs[GROUP : GROUP + arrivals], refs[GROUP + arrivals :]
    for at in range(0, owns[0].shape[0], HALF):
        for c in range(GROUP):
            value = owns[c][at : at + HALF, :]
            for ref in arrived:
                value = value + decode(ref[c, at : at + HALF, :])
            outs[c][at : at + HALF, :] = encode(value) if outs[c].dtype == jnp.int16 else value


def merge_kernel(own_ref, *refs, arrivals, far, pairs):
    own_out = refs[arrivals]
    outs = refs[arrivals + 1 :]
    for z in range(far):
        for pair in range(pairs):
            at = pl.ds((z * pairs + pair) * HALF, HALF)
            total = own_ref[at, :]
            for ref in refs[:arrivals]:
                total = total + decode(ref[at, :])
            to = pl.ds(pair * HALF, HALF)
            if z == 0:
                own_out[to, :] = total
            else:
                outs[z - 1][to, :] = encode(total)


def finish_kernel(members_ref, own_ref, *refs, arrivals, pairs, scale):
    out_ref = refs[arrivals]
    baselines = members_ref.shape[1]
    first = members_ref[0:1, :]
    second = members_ref[1:2, :]
    rising = first < second
    station = iota((HALF, baselines), 0)
    for pair in range(pairs):
        at = pl.ds(pair * HALF, HALF)
        total = own_ref[at, :]
        for ref in refs[:arrivals]:
            total = total + decode(ref[at, :])
        total = total * scale
        total = jnp.where(iota(total.shape, 0) < 60, total, 0.0)
        flipped = total.T
        coarse = flipped.astype(jnp.bfloat16)
        medium = (flipped - coarse.astype(jnp.float32)).astype(jnp.bfloat16)
        stack = jnp.concatenate([coarse, medium], axis=0)
        picked = {}
        for side, members in enumerate((first, second)):
            for p in range(2):
                choose = (station == 2 * members + p).astype(jnp.bfloat16)
                rows = jnp.dot(stack, choose, preferred_element_type=jnp.float32)
                rows = rows[:LANES] + rows[LANES:]
                partner = second if side == 0 else first
                for half in range(2):
                    for p2 in range(2):
                        match = station == 2 * partner + p2
                        part = rows[half * HALF : (half + 1) * HALF]
                        picked[side, half, p, p2] = jnp.sum(
                            jnp.where(match, part, 0.0), axis=0, keepdims=True
                        )
        for half in range(2):
            real, imaginary = [], []
            for p in range(2):
                for p2 in range(2):
                    a = picked[0, half, p, p2]
                    b = picked[1, half, p2, p]
                    real.append(jnp.where(rising, a, b))
                    imaginary.append(jnp.where(rising, b, -a))
            out_ref[2 * pair + half, 0] = jnp.concatenate(real, axis=0)
            out_ref[2 * pair + half, 1] = jnp.concatenate(imaginary, axis=0)


def on_device(volts, entry, turning, members, target, *, tm, chips):
    near = max(1, chips // 4)
    far = chips // near
    fine = turning.shape[1]
    spectra = volts.shape[1]
    centres = entry.shape[1]
    per_device = Q // (2 * chips)
    pairs = per_device // 2
    channels = volts.shape[4]

    def across_chips(x, step):
        return lax.ppermute(x, "chip", [(i, i ^ step) for i in range(chips)])

    def across_cores(x):
        return lax.ppermute(x, "core", [(0, 1), (1, 0)])

    chip = lax.axis_index("chip")
    core = lax.axis_index("core")
    x = lax.axis_index("tm")
    place = [value.astype(jnp.int32).reshape(1) for value in (chip, core, x)]
    other = across_cores(volts)
    block = pl.pallas_call(
        pack_kernel,
        in_specs=[HBM, HBM],
        out_specs=VMEM,
        out_shape=jax.ShapeDtypeStruct((fine // 2 + 16, LANES), jnp.int16),
        scratch_shapes=[
            pltpu.VMEM(turning.shape, jnp.float32),
            pltpu.VMEM((fine // LANES, LANES), jnp.int32),
            pltpu.SemaphoreType.DMA((2,)),
        ],
        compiler_params=params(56),
        cost_estimate=cost(1),
        name="pack",
    )(turning, target.reshape(fine // LANES, LANES))
    line = [block] + [across_chips(block, z * near) for z in range(1, far)]

    pitch = 2 * spectra + 1
    held_type = pltpu.VMEM((channels * pitch + ROW, LANES), jnp.float32)

    def rows(side, *operands):
        return pl.pallas_call(
            functools.partial(rows_kernel, first=side * spectra, pitch=pitch),
            in_specs=[HBM, SMEM, SMEM, SMEM, VMEM][: 4 + side],
            out_specs=VMEM,
            out_shape=held_type,
            scratch_shapes=[
                pltpu.VMEM((channels // WIDTH, 2, spectra, 32, 2, WIDTH), jnp.bfloat16),
                pltpu.SemaphoreType.DMA((channels // WIDTH,)),
            ],
            input_output_aliases={4: 0} if side else {},
            compiler_params=params(40),
            cost_estimate=cost(5),
            name="rows",
        )(*operands)

    held = rows(0, volts, *place)
    size = block.shape[0]
    stack = pl.pallas_call(
        stack_kernel,
        in_specs=[ANY] + [VMEM] * far,
        out_specs=VMEM,
        out_shape=jax.ShapeDtypeStruct((far * size, LANES), jnp.int16),
        compiler_params=params(4),
        cost_estimate=cost(1),
        name="stack",
    )(held, *line)
    mine = [stack] + [across_chips(stack, y) for y in range(1, near)]
    theirs = [across_cores(stack)]
    held = rows(1, other, *place, held)
    each = far * pairs
    arrived = []
    after = entry
    for group in range(centres // GROUP):
        state = ()
        for part in range(3 if near > 1 else 1):
            if part == 0:
                columns = [(0, False), (0, True)]
            else:
                columns = [(y, part == 2) for y in range(1, near)]
            if part == 1 and group == 0:
                state, mine = lax.optimization_barrier((state, mine))
                theirs += [across_cores(value) for value in mine[1:]]
            stacks = [(theirs if across else mine)[y] for y, across in columns]
            held, *state, source = pl.pallas_call(
                functools.partial(
                    prepare_kernel,
                    columns=columns,
                    started=part > 0,
                    group=group,
                    near=near,
                    far=far,
                    per=per_device,
                    fine=fine,
                    pitch=pitch,
                ),
                in_specs=[SMEM, SMEM, SMEM, VMEM, ANY] + [VMEM] * (1 + len(stacks) + len(state)),
                out_specs=[VMEM] * 4,
                out_shape=[
                    held_type,
                    jax.ShapeDtypeStruct((Q // 2, LANES), jnp.float32),
                    jax.ShapeDtypeStruct((Q, LANES), jnp.float32),
                    jax.ShapeDtypeStruct((Q // 2, LANES), jnp.int32),
                ],
                input_output_aliases={5: 0},
                compiler_params=params(16),
                cost_estimate=cost(2),
                name="prepare",
            )(*place, entry, after, held, *stacks, *state)
        def correlate(first_pair, out_types, source=source, held=held):
            return pl.pallas_call(
                functools.partial(
                    correlate_kernel,
                    first_pair=first_pair,
                    pairs=each,
                    spectra=spectra,
                    sent=len(out_types) == 1,
                ),
                in_specs=[SMEM, VMEM],
                out_specs=[VMEM] * len(out_types),
                out_shape=out_types,
                scratch_shapes=[
                    pltpu.VMEM((LANES * ROW, LANES), jnp.float32),
                    pltpu.VMEM((LANES * ROW, LANES), jnp.float32),
                    pltpu.VMEM((GROUP, 2 * LANES, 2 * spectra * LANES), jnp.bfloat16),
                    pltpu.VMEM((GROUP, 2 * LANES, 2 * spectra * LANES), jnp.bfloat16),
                    pltpu.VMEM((GROUP, HALF, LANES), jnp.float32),
                ]
                + [pltpu.VMEM((each * HALF, LANES), jnp.float32)] * (GROUP if len(out_types) == 1 else 0),
                compiler_params=params(12),
                cost_estimate=cost(9),
                name="correlate",
            )(source, held)

        columns_in = []
        for y in range(1, near):
            sent = correlate(
                y * each, [jax.ShapeDtypeStruct((GROUP, each * HALF, LANES), jnp.int16)]
            )[0]
            columns_in.append(across_chips(sent, y))
        own = correlate(0, [jax.ShapeDtypeStruct((each * HALF, LANES), jnp.float32)] * GROUP)
        after = own[0]
        if columns_in:
            kinds = [jnp.int16 if group + c else jnp.float32 for c in range(GROUP)]
            own = pl.pallas_call(
                functools.partial(join_kernel, arrivals=len(columns_in)),
                in_specs=[VMEM] * (GROUP + len(columns_in)),
                out_specs=[VMEM] * GROUP,
                out_shape=[jax.ShapeDtypeStruct((each * HALF, LANES), kind) for kind in kinds],
                compiler_params=params(8),
                cost_estimate=cost(1),
                name="join",
            )(*own, *columns_in)
        for c in range(GROUP):
            centre = group * GROUP + c
            if centre == 0:
                total = own[c]
            else:
                arrived.append(
                    lax.ppermute(own[c], "tm", [(i, i ^ centre) for i in range(tm)])
                )
    rows = pairs * HALF
    merged = pl.pallas_call(
        functools.partial(merge_kernel, arrivals=len(arrived), far=far, pairs=pairs),
        in_specs=[VMEM] * (1 + len(arrived)),
        out_specs=[VMEM] * far,
        out_shape=[
            jax.ShapeDtypeStruct((rows, LANES), jnp.int16 if z else jnp.float32)
            for z in range(far)
        ],
        compiler_params=params(6),
        cost_estimate=cost(1),
        name="merge",
    )(total, *arrived)
    final = [across_chips(merged[z], z * near) for z in range(1, far)]
    return pl.pallas_call(
        functools.partial(finish_kernel, arrivals=len(final), pairs=pairs, scale=Q / channels),
        in_specs=[VMEM] * (2 + len(final)),
        out_specs=VMEM,
        out_shape=jax.ShapeDtypeStruct((per_device, 2, 4, members.shape[0]), jnp.float32),
        compiler_params=params(6),
        cost_estimate=cost(2),
        name="finish",
    )(members.T, merged[0], *final)


def solution(mesh):
    tm = mesh.shape["tm"]
    chips = mesh.shape["chan"] // 2
    inner = Mesh(mesh.devices.reshape(tm, chips, 2), ("tm", "chip", "core"))
    every = ("tm", "chip", "core")
    split = ("chip", "core")
    return jax.shard_map(
        functools.partial(on_device, tm=tm, chips=chips),
        mesh=inner,
        in_specs=(
            P(None, every, None, None, None),
            P("tm", None, None),
            P(None, split),
            P(),
            P(split),
        ),
        out_specs=P(every, None, None, None),
        check_vma=False,
    )
```

```python
import functools

import jax
import jax.numpy as jnp
import numpy as np
from jax import lax
from jax.experimental import pallas as pl
from jax.experimental.pallas import tpu as pltpu
from jax.sharding import Mesh
from jax.sharding import PartitionSpec as P

Q = 64
LANES = 128
HALF = 64
WIDTH = 1024
ROW = 8
GROUP = 2
TURN = 65536.0
COSINE = (-0.9999992251396179, 19.738981246948242, -64.92865753173828, 85.27162170410156, -58.79049301147461, 21.07110595703125)
VMEM = pl.BlockSpec(memory_space=pltpu.VMEM)
SMEM = pl.BlockSpec(memory_space=pltpu.SMEM)
ANY = pl.BlockSpec(memory_space=pl.ANY)
HBM = pl.BlockSpec(memory_space=pltpu.HBM)


def iota(shape, dim):
    return lax.broadcasted_iota(jnp.int32, shape, dim)


def params(mib):
    return pltpu.CompilerParams(vmem_limit_bytes=mib * 1024 * 1024)


def cost(microseconds):
    return pl.CostEstimate(
        flops=int(microseconds * 1.0e9), bytes_accessed=int(microseconds * 3.0e6), transcendentals=0
    )


def pack_kernel(turning_hbm, bins_hbm, out_ref, turning_ref, bins_ref, sems):
    entries, fine = turning_ref.shape
    rows = fine // 2
    copies = [
        pltpu.make_async_copy(turning_hbm, turning_ref, sems.at[0]),
        pltpu.make_async_copy(bins_hbm, bins_ref, sems.at[1]),
    ]
    for copy in copies:
        copy.start()
    for copy in copies:
        copy.wait()
    codes = jnp.round(turning_ref[...] * (TURN / (2.0 * np.pi)))
    flipped = codes.T
    pair = jnp.concatenate([flipped[:rows], flipped[rows:]], axis=1)
    out_ref[0:rows, :] = pair.astype(jnp.int32).astype(jnp.int16)
    spare = jnp.zeros((out_ref.shape[0] - rows - bins_ref.shape[0], LANES), jnp.int32)
    out_ref[rows:, :] = jnp.concatenate([bins_ref[...], spare], axis=0).astype(jnp.int16)


def stack_kernel(after_ref, *refs):
    del after_ref
    out_ref = refs[-1]
    size = refs[0].shape[0]
    for k, ref in enumerate(refs[:-1]):
        out_ref[k * size : (k + 1) * size, :] = ref[...]


def encode(block):
    top = jnp.max(jnp.max(jnp.abs(block), axis=0, keepdims=True), axis=1, keepdims=True)
    power = jnp.floor(jnp.log2(jnp.maximum(top, 1e-30)))
    code = jnp.clip(jnp.round(block * jnp.exp2(14.0 - power)), -32767.0, 32767.0)
    code = jnp.where(iota(block.shape, 0) == 60, power, code)
    return code.astype(jnp.int32).astype(jnp.int16)


def decode(code):
    code = code.astype(jnp.int32).astype(jnp.float32)
    scale = jnp.exp2(code[60:61, 0:1] - 14.0)
    return code * scale


def rows_kernel(volts_ref, *rest, first, pitch):
    held, raw, sems = rest[-3:]
    parts, spectra, stations = volts_ref.shape[:3]
    width = raw.shape[-1]
    steps = raw.shape[0]
    unroll = 2

    def fetch(step):
        return pltpu.make_async_copy(
            volts_ref.at[:, :, :, :, pl.ds(pl.multiple_of(step * width, width), width)],
            raw.at[step, :, :, pl.ds(0, stations)],
            sems.at[step],
        )

    def start(step, _):
        raw[step, :, :, stations:] = jnp.zeros(
            (parts, spectra, raw.shape[3] - stations, 2, width), jnp.bfloat16
        )
        fetch(step).start()
        return 0

    lax.fori_loop(0, steps, start, 0)

    def flip(group, _):
        for unit in range(unroll):
            fetch(group * unroll + unit).wait()
        for unit in range(unroll):
            step = group * unroll + unit
            for k in range(width // LANES):
                block = raw[step, :, :, :, :, k * LANES : (k + 1) * LANES]
                block = block.reshape(parts * spectra * HALF, LANES)
                for t in range(spectra):
                    both = jnp.concatenate(
                        [
                            block[(part * spectra + t) * HALF : (part * spectra + t + 1) * HALF]
                            for part in range(parts)
                        ],
                        axis=0,
                    )
                    at = (step * width + k * LANES) * pitch + first + t
                    held[pl.ds(at, LANES, stride=pitch), :] = both.astype(jnp.float32).T
        return 0

    lax.fori_loop(0, steps // unroll, flip, 0)


def prepare_kernel(
    chip_ref, core_ref, x_ref, entry_ref, after_ref, held_in, *rest, columns, started, group, near, far, per, fine, pitch
):
    del after_ref, held_in
    stacks = rest[: len(columns)]
    rest = rest[len(columns) :]
    if started:
        carry_in, found_in = rest[:2]
        rest = rest[2:]
    held, carry_ref, found_ref, source_ref = rest
    chip = chip_ref[0]
    core = core_ref[0]
    x = x_ref[0]
    q_here = source_ref.shape[0]
    per_bits = per.bit_length() - 1
    near_bits = near.bit_length() - 1
    size = fine // 2 + 16
    blocks = [
        (stack, z * size, (chip ^ (z * near + column)) * 2 + (1 - core if other else core))
        for stack, (column, other) in zip(stacks, columns)
        for z in range(far)
    ]

    stations = entry_ref.shape[2]
    twice = (iota((stations, HALF), 0) == (iota((stations, HALF), 1) >> 1)).astype(jnp.bfloat16)
    entries = jnp.concatenate(
        [
            jnp.dot(
                entry_ref[0, pl.ds((group * GROUP + c) ^ x, 1), :]
                .astype(jnp.float32)
                .astype(jnp.bfloat16),
                twice,
                preferred_element_type=jnp.float32,
            )
            for c in range(GROUP)
        ],
        axis=1,
    ).astype(jnp.int32)
    row = iota((2 * LANES, LANES), 0)
    weight = jnp.where(row < LANES, 2.0**-8, 2.0**-16)
    spread = jnp.concatenate(
        [
            jnp.where(
                ((row & (HALF - 1)) == entries) & (((row >> 6) & 1) == half), weight, 0.0
            ).astype(jnp.bfloat16)
            for half in range(2)
        ],
        axis=1,
    )
    code = jnp.concatenate([stack[at : at + fine // 2, :] for stack, at, _ in blocks], axis=0)
    code = code.astype(jnp.int32).astype(jnp.float32)
    high = jnp.floor(code * (1.0 / 256.0))
    digits = jnp.concatenate([high, code - 256.0 * high], axis=1).astype(jnp.bfloat16)
    turns = jnp.dot(digits, spread, preferred_element_type=jnp.float32)
    for index, (_, _, owner) in enumerate(blocks):
        for half in range(2):
            at = (owner * 2 + half) * (fine // 2) * pitch + pitch - 1
            held[pl.ds(at, fine // 2, stride=pitch), :] = turns[
                index * (fine // 2) : (index + 1) * (fine // 2), half * LANES : (half + 1) * LANES
            ]

    if started:
        carry = carry_in[:, 0:1]
        found = found_in[...]
    else:
        carry = jnp.zeros((q_here, 1), jnp.float32)
        found = jnp.zeros((2 * q_here, LANES), jnp.float32)
    lane = iota((q_here, fine), 1)
    hits = []
    for stack, at, _ in blocks:
        tail = stack[at + fine // 2 : at + size, :].astype(jnp.int32)
        bins = jnp.concatenate([tail[r : r + 1, :] for r in range(fine // LANES)], axis=1)
        bin_owner = bins >> per_bits
        relative = (bin_owner >> 1) ^ chip
        label = ((relative & (near - 1)) * far + (relative >> near_bits)) * per
        label = label + (bins & (per - 1))
        label = jnp.where((bin_owner & 1) == core, label, -1)
        hits.append(jnp.where(iota((q_here, fine), 0) == label, 1.0, 0.0))
    above = (iota((fine, fine), 0) < iota((fine, fine), 1)).astype(jnp.bfloat16)
    every = jnp.concatenate(hits, axis=0).astype(jnp.bfloat16)
    every = jnp.dot(every, above, preferred_element_type=jnp.float32)
    ids, at_rank = [], []
    for index, (hit, (_, _, owner)) in enumerate(zip(hits, blocks)):
        before = every[index * q_here : (index + 1) * q_here]
        rank = jnp.sum(hit * (before + carry), axis=0, keepdims=True)
        carry = carry + before[:, fine - 1 : fine] + hit[:, fine - 1 : fine]
        at_rank.append((iota((LANES, fine), 0) == rank.astype(jnp.int32)).astype(jnp.bfloat16))
        high = hit * (owner * (fine // LANES) + (lane >> 7)).astype(jnp.float32)
        low = hit * (lane & (LANES - 1)).astype(jnp.float32)
        ids.append(jnp.concatenate([high, low], axis=0).astype(jnp.bfloat16))
    found = found + lax.dot_general(
        jnp.concatenate(ids, axis=1),
        jnp.concatenate(at_rank, axis=1),
        (((1,), (1,)), ((), ())),
        preferred_element_type=jnp.float32,
    )
    carry_ref[...] = jnp.broadcast_to(carry, carry_ref.shape)
    found_ref[...] = found
    source_ref[...] = ((found[:q_here] * LANES + found[q_here:]) * pitch).astype(jnp.int32)


def wave(z):
    value = jnp.full_like(z, COSINE[-1])
    for coefficient in COSINE[-2::-1]:
        value = value * z + coefficient
    return value


def correlate_kernel(source_ref, held, *rest, first_pair, pairs, spectra, sent):
    outs = rest[: 1 if sent else GROUP]
    rest = rest[len(outs) :]
    even, odd, wide_even, wide_odd, kept = rest[:5]
    sums = rest[5:] if sent else outs

    def gather(unit, into):
        for first in range(0, LANES, 32):
            at = [source_ref[unit, first + k] for k in range(32)]
            rows = [held[pl.ds(a, ROW), :] for a in at]
            for k in range(32):
                into[(first + k) * ROW : (first + k + 1) * ROW, :] = rows[k]

    upper = (iota((HALF, LANES), 1) & (HALF - 1)) > iota((HALF, LANES), 0)
    left = iota((HALF, LANES), 1) < HALF

    def rotate(rows, wide):
        turns = rows[pl.ds(2 * spectra, LANES, stride=ROW), :].T
        turning = []
        for centre in range(GROUP):
            angle = turns[centre * HALF : (centre + 1) * HALF]
            cosine = jnp.abs(angle) - 0.5
            sine = jnp.abs(angle - 0.25) - 0.5
            turning.append((wave(cosine * cosine), wave(sine * sine)))
        for t in range(2 * spectra):
            volts = rows[pl.ds(t, LANES, stride=ROW), :].T
            real, imaginary = volts[:HALF], volts[HALF:]
            columns = slice(t * LANES, (t + 1) * LANES)
            for centre in range(GROUP):
                cosine, sine = turning[centre]
                rotated = (real * cosine + imaginary * sine, imaginary * cosine - real * sine)
                for part, value in enumerate(rotated):
                    coarse = value.astype(jnp.bfloat16)
                    rest_of = (value - coarse.astype(jnp.float32)).astype(jnp.bfloat16)
                    wide[centre, part * HALF : (part + 1) * HALF, columns] = coarse
                    wide[centre, LANES + part * HALF : LANES + (part + 1) * HALF, columns] = rest_of

    def correlate(wide):
        results = []
        for centre in range(GROUP):
            product = lax.dot_general(
                wide[centre],
                wide[centre, :LANES],
                (((1,), (1,)), ((), ())),
                preferred_element_type=jnp.float32,
            )
            product = product[:LANES] + product[LANES:]
            under = pltpu.roll(product[HALF:], HALF, 1)
            results.append(product[:HALF] + jnp.where(left, under, -under))
        return results

    def emit(pair, seconds):
        for centre in range(GROUP):
            first, second = kept[centre], seconds[centre]
            first = jnp.where(upper, first, pltpu.roll(first, HALF, 1))
            second = jnp.where(upper, pltpu.roll(second, HALF, 1), second)
            value = jnp.where(left, first, second)
            at = pl.ds(pl.multiple_of(pair * HALF, HALF), HALF)
            sums[centre][at, :] = value

    base = 2 * first_pair
    last = base + 2 * pairs - 1
    gather(base, even)

    def one(pair, _):
        unit = base + 2 * pair
        gather(unit + 1, odd)
        rotate(even, wide_even)
        emit(jnp.maximum(pair - 1, 0), correlate(wide_odd))
        gather(jnp.minimum(unit + 2, last), even)
        rotate(odd, wide_odd)
        for centre, value in enumerate(correlate(wide_even)):
            kept[centre] = value
        return 0

    lax.fori_loop(0, pairs, one, 0)
    emit(pairs - 1, correlate(wide_odd))
    if sent:
        for centre in range(GROUP):
            for pair in range(pairs):
                at = slice(pair * HALF, (pair + 1) * HALF)
                outs[0][centre, at, :] = encode(sums[centre][at, :])


def join_kernel(*refs, arrivals):
    owns, arrived, outs = refs[:GROUP], refs[GROUP : GROUP + arrivals], refs[GROUP + arrivals :]
    for at in range(0, owns[0].shape[0], HALF):
        for c in range(GROUP):
            value = owns[c][at : at + HALF, :]
            for ref in arrived:
                value = value + decode(ref[c, at : at + HALF, :])
            outs[c][at : at + HALF, :] = encode(value) if outs[c].dtype == jnp.int16 else value


def merge_kernel(own_ref, *refs, arrivals, far, pairs):
    own_out = refs[arrivals]
    outs = refs[arrivals + 1 :]
    for z in range(far):
        for pair in range(pairs):
            at = pl.ds((z * pairs + pair) * HALF, HALF)
            total = own_ref[at, :]
            for ref in refs[:arrivals]:
                total = total + decode(ref[at, :])
            to = pl.ds(pair * HALF, HALF)
            if z == 0:
                own_out[to, :] = total
            else:
                outs[z - 1][to, :] = encode(total)


def finish_kernel(members_ref, own_ref, *refs, arrivals, pairs, scale):
    out_ref = refs[arrivals]
    baselines = members_ref.shape[1]
    first = members_ref[0:1, :]
    second = members_ref[1:2, :]
    rising = first < second
    station = iota((HALF, baselines), 0)
    for pair in range(pairs):
        at = pl.ds(pair * HALF, HALF)
        total = own_ref[at, :]
        for ref in refs[:arrivals]:
            total = total + decode(ref[at, :])
        total = total * scale
        total = jnp.where(iota(total.shape, 0) < 60, total, 0.0)
        flipped = total.T
        coarse = flipped.astype(jnp.bfloat16)
        medium = (flipped - coarse.astype(jnp.float32)).astype(jnp.bfloat16)
        stack = jnp.concatenate([coarse, medium], axis=0)
        picked = {}
        for side, members in enumerate((first, second)):
            for p in range(2):
                choose = (station == 2 * members + p).astype(jnp.bfloat16)
                rows = jnp.dot(stack, choose, preferred_element_type=jnp.float32)
                rows = rows[:LANES] + rows[LANES:]
                partner = second if side == 0 else first
                for half in range(2):
                    for p2 in range(2):
                        match = station == 2 * partner + p2
                        part = rows[half * HALF : (half + 1) * HALF]
                        picked[side, half, p, p2] = jnp.sum(
                            jnp.where(match, part, 0.0), axis=0, keepdims=True
                        )
        for half in range(2):
            real, imaginary = [], []
            for p in range(2):
                for p2 in range(2):
                    a = picked[0, half, p, p2]
                    b = picked[1, half, p2, p]
                    real.append(jnp.where(rising, a, b))
                    imaginary.append(jnp.where(rising, b, -a))
            out_ref[2 * pair + half, 0] = jnp.concatenate(real, axis=0)
            out_ref[2 * pair + half, 1] = jnp.concatenate(imaginary, axis=0)


def on_device(volts, entry, turning, members, target, *, tm, chips):
    near = max(1, chips // 4)
    far = chips // near
    fine = turning.shape[1]
    spectra = volts.shape[1]
    centres = entry.shape[1]
    per_device = Q // (2 * chips)
    pairs = per_device // 2
    channels = volts.shape[4]

    def across_chips(x, step):
        return lax.ppermute(x, "chip", [(i, i ^ step) for i in range(chips)])

    def across_cores(x):
        return lax.ppermute(x, "core", [(0, 1), (1, 0)])

    chip = lax.axis_index("chip")
    core = lax.axis_index("core")
    x = lax.axis_index("tm")
    place = [value.astype(jnp.int32).reshape(1) for value in (chip, core, x)]
    other = across_cores(volts)
    block = pl.pallas_call(
        pack_kernel,
        in_specs=[HBM, HBM],
        out_specs=VMEM,
        out_shape=jax.ShapeDtypeStruct((fine // 2 + 16, LANES), jnp.int16),
        scratch_shapes=[
            pltpu.VMEM(turning.shape, jnp.float32),
            pltpu.VMEM((fine // LANES, LANES), jnp.int32),
            pltpu.SemaphoreType.DMA((2,)),
        ],
        compiler_params=params(56),
        cost_estimate=cost(1),
        name="pack",
    )(turning, target.reshape(fine // LANES, LANES))
    line = [block] + [across_chips(block, z * near) for z in range(1, far)]

    pitch = 2 * spectra + 1
    held_type = pltpu.VMEM((channels * pitch + ROW, LANES), jnp.float32)

    def rows(side, *operands):
        return pl.pallas_call(
            functools.partial(rows_kernel, first=side * spectra, pitch=pitch),
            in_specs=[HBM, SMEM, SMEM, SMEM, VMEM][: 4 + side],
            out_specs=VMEM,
            out_shape=held_type,
            scratch_shapes=[
                pltpu.VMEM((channels // WIDTH, 2, spectra, 32, 2, WIDTH), jnp.bfloat16),
                pltpu.SemaphoreType.DMA((channels // WIDTH,)),
            ],
            input_output_aliases={4: 0} if side else {},
            compiler_params=params(40),
            cost_estimate=cost(5),
            name="rows",
        )(*operands)

    held = rows(0, volts, *place)
    size = block.shape[0]
    stack = pl.pallas_call(
        stack_kernel,
        in_specs=[ANY] + [VMEM] * far,
        out_specs=VMEM,
        out_shape=jax.ShapeDtypeStruct((far * size, LANES), jnp.int16),
        compiler_params=params(4),
        cost_estimate=cost(1),
        name="stack",
    )(held, *line)
    mine = [stack] + [across_chips(stack, y) for y in range(1, near)]
    theirs = [across_cores(stack)]
    held = rows(1, other, *place, held)
    each = far * pairs
    arrived = []
    after = entry
    for group in range(centres // GROUP):
        state = ()
        for part in range(3 if near > 1 else 1):
            if part == 0:
                columns = [(0, False), (0, True)]
            else:
                columns = [(y, part == 2) for y in range(1, near)]
            if part == 1 and group == 0:
                state, mine = lax.optimization_barrier((state, mine))
                theirs += [across_cores(value) for value in mine[1:]]
            stacks = [(theirs if across else mine)[y] for y, across in columns]
            held, *state, source = pl.pallas_call(
                functools.partial(
                    prepare_kernel,
                    columns=columns,
                    started=part > 0,
                    group=group,
                    near=near,
                    far=far,
                    per=per_device,
                    fine=fine,
                    pitch=pitch,
                ),
                in_specs=[SMEM, SMEM, SMEM, VMEM, ANY] + [VMEM] * (1 + len(stacks) + len(state)),
                out_specs=[VMEM] * 4,
                out_shape=[
                    held_type,
                    jax.ShapeDtypeStruct((Q // 2, LANES), jnp.float32),
                    jax.ShapeDtypeStruct((Q, LANES), jnp.float32),
                    jax.ShapeDtypeStruct((Q // 2, LANES), jnp.int32),
                ],
                input_output_aliases={5: 0},
                compiler_params=params(16),
                cost_estimate=cost(2),
                name="prepare",
            )(*place, entry, after, held, *stacks, *state)
        def correlate(first_pair, out_types, source=source, held=held):
            return pl.pallas_call(
                functools.partial(
                    correlate_kernel,
                    first_pair=first_pair,
                    pairs=each,
                    spectra=spectra,
                    sent=len(out_types) == 1,
                ),
                in_specs=[SMEM, VMEM],
                out_specs=[VMEM] * len(out_types),
                out_shape=out_types,
                scratch_shapes=[
                    pltpu.VMEM((LANES * ROW, LANES), jnp.float32),
                    pltpu.VMEM((LANES * ROW, LANES), jnp.float32),
                    pltpu.VMEM((GROUP, 2 * LANES, 2 * spectra * LANES), jnp.bfloat16),
                    pltpu.VMEM((GROUP, 2 * LANES, 2 * spectra * LANES), jnp.bfloat16),
                    pltpu.VMEM((GROUP, HALF, LANES), jnp.float32),
                ]
                + [pltpu.VMEM((each * HALF, LANES), jnp.float32)] * (GROUP if len(out_types) == 1 else 0),
                compiler_params=params(12),
                cost_estimate=cost(9),
                name="correlate",
            )(source, held)

        columns_in = []
        for y in range(1, near):
            sent = correlate(
                y * each, [jax.ShapeDtypeStruct((GROUP, each * HALF, LANES), jnp.int16)]
            )[0]
            columns_in.append(across_chips(sent, y))
        own = correlate(0, [jax.ShapeDtypeStruct((each * HALF, LANES), jnp.float32)] * GROUP)
        after = own[0]
        if columns_in:
            kinds = [jnp.int16 if group + c else jnp.float32 for c in range(GROUP)]
            own = pl.pallas_call(
                functools.partial(join_kernel, arrivals=len(columns_in)),
                in_specs=[VMEM] * (GROUP + len(columns_in)),
                out_specs=[VMEM] * GROUP,
                out_shape=[jax.ShapeDtypeStruct((each * HALF, LANES), kind) for kind in kinds],
                compiler_params=params(8),
                cost_estimate=cost(1),
                name="join",
            )(*own, *columns_in)
        for c in range(GROUP):
            centre = group * GROUP + c
            if centre == 0:
                total = own[c]
            else:
                arrived.append(
                    lax.ppermute(own[c], "tm", [(i, i ^ centre) for i in range(tm)])
                )
    rows = pairs * HALF
    merged = pl.pallas_call(
        functools.partial(merge_kernel, arrivals=len(arrived), far=far, pairs=pairs),
        in_specs=[VMEM] * (1 + len(arrived)),
        out_specs=[VMEM] * far,
        out_shape=[
            jax.ShapeDtypeStruct((rows, LANES), jnp.int16 if z else jnp.float32)
            for z in range(far)
        ],
        compiler_params=params(6),
        cost_estimate=cost(1),
        name="merge",
    )(total, *arrived)
    final = [across_chips(merged[z], z * near) for z in range(far - 1, 0, -1)]
    return pl.pallas_call(
        functools.partial(finish_kernel, arrivals=len(final), pairs=pairs, scale=Q / channels),
        in_specs=[VMEM] * (2 + len(final)),
        out_specs=VMEM,
        out_shape=jax.ShapeDtypeStruct((per_device, 2, 4, members.shape[0]), jnp.float32),
        compiler_params=params(6),
        cost_estimate=cost(2),
        name="finish",
    )(members.T, merged[0], *final)


def solution(mesh):
    tm = mesh.shape["tm"]
    chips = mesh.shape["chan"] // 2
    inner = Mesh(mesh.devices.reshape(tm, chips, 2), ("tm", "chip", "core"))
    every = ("tm", "chip", "core")
    split = ("chip", "core")
    return jax.shard_map(
        functools.partial(on_device, tm=tm, chips=chips),
        mesh=inner,
        in_specs=(
            P(None, every, None, None, None),
            P("tm", None, None),
            P(None, split),
            P(),
            P(split),
        ),
        out_specs=P(every, None, None, None),
        check_vma=False,
    )
```

```python
import functools

import jax
import jax.numpy as jnp
import numpy as np
from jax import lax
from jax.experimental import pallas as pl
from jax.experimental.pallas import tpu as pltpu
from jax.sharding import Mesh
from jax.sharding import PartitionSpec as P

Q = 64
LANES = 128
HALF = 64
WIDTH = 1024
ROW = 8
GROUP = 2
TURN = 65536.0
COSINE = (-0.9999992251396179, 19.738981246948242, -64.92865753173828, 85.27162170410156, -58.79049301147461, 21.07110595703125)
VMEM = pl.BlockSpec(memory_space=pltpu.VMEM)
SMEM = pl.BlockSpec(memory_space=pltpu.SMEM)
ANY = pl.BlockSpec(memory_space=pl.ANY)
HBM = pl.BlockSpec(memory_space=pltpu.HBM)


def iota(shape, dim):
    return lax.broadcasted_iota(jnp.int32, shape, dim)


def params(mib):
    return pltpu.CompilerParams(vmem_limit_bytes=mib * 1024 * 1024)


def cost(microseconds):
    return pl.CostEstimate(
        flops=int(microseconds * 1.0e9), bytes_accessed=int(microseconds * 3.0e6), transcendentals=0
    )


def pack_kernel(turning_hbm, bins_hbm, out_ref, turning_ref, bins_ref, sems):
    entries, fine = turning_ref.shape
    rows = fine // 2
    copies = [
        pltpu.make_async_copy(turning_hbm, turning_ref, sems.at[0]),
        pltpu.make_async_copy(bins_hbm, bins_ref, sems.at[1]),
    ]
    for copy in copies:
        copy.start()
    for copy in copies:
        copy.wait()
    codes = jnp.round(turning_ref[...] * (TURN / (2.0 * np.pi)))
    flipped = codes.T
    pair = jnp.concatenate([flipped[:rows], flipped[rows:]], axis=1)
    out_ref[0:rows, :] = pair.astype(jnp.int32).astype(jnp.int16)
    spare = jnp.zeros((out_ref.shape[0] - rows - bins_ref.shape[0], LANES), jnp.int32)
    out_ref[rows:, :] = jnp.concatenate([bins_ref[...], spare], axis=0).astype(jnp.int16)


def stack_kernel(after_ref, *refs):
    del after_ref
    out_ref = refs[-1]
    size = refs[0].shape[0]
    for k, ref in enumerate(refs[:-1]):
        out_ref[k * size : (k + 1) * size, :] = ref[...]


def encode(block):
    top = jnp.max(jnp.max(jnp.abs(block), axis=0, keepdims=True), axis=1, keepdims=True)
    power = jnp.floor(jnp.log2(jnp.maximum(top, 1e-30)))
    code = jnp.clip(jnp.round(block * jnp.exp2(14.0 - power)), -32767.0, 32767.0)
    code = jnp.where(iota(block.shape, 0) == 60, power, code)
    return code.astype(jnp.int32).astype(jnp.int16)


def decode(code):
    code = code.astype(jnp.int32).astype(jnp.float32)
    scale = jnp.exp2(code[60:61, 0:1] - 14.0)
    return code * scale


def rows_kernel(volts_ref, *rest, first, pitch):
    held, raw, sems = rest[-3:]
    parts, spectra, stations = volts_ref.shape[:3]
    width = raw.shape[-1]
    steps = raw.shape[0]
    unroll = 2

    def fetch(step):
        return pltpu.make_async_copy(
            volts_ref.at[:, :, :, :, pl.ds(pl.multiple_of(step * width, width), width)],
            raw.at[step, :, :, pl.ds(0, stations)],
            sems.at[step],
        )

    def start(step, _):
        raw[step, :, :, stations:] = jnp.zeros(
            (parts, spectra, raw.shape[3] - stations, 2, width), jnp.bfloat16
        )
        fetch(step).start()
        return 0

    lax.fori_loop(0, steps, start, 0)

    def flip(group, _):
        for unit in range(unroll):
            fetch(group * unroll + unit).wait()
        for unit in range(unroll):
            step = group * unroll + unit
            for k in range(width // LANES):
                block = raw[step, :, :, :, :, k * LANES : (k + 1) * LANES]
                block = block.reshape(parts * spectra * HALF, LANES)
                for t in range(spectra):
                    both = jnp.concatenate(
                        [
                            block[(part * spectra + t) * HALF : (part * spectra + t + 1) * HALF]
                            for part in range(parts)
                        ],
                        axis=0,
                    )
                    at = (step * width + k * LANES) * pitch + first + t
                    held[pl.ds(at, LANES, stride=pitch), :] = both.astype(jnp.float32).T
        return 0

    lax.fori_loop(0, steps // unroll, flip, 0)


def prepare_kernel(
    chip_ref, core_ref, x_ref, entry_ref, after_ref, held_in, *rest, columns, started, group, near, far, per, fine, pitch
):
    del after_ref, held_in
    stacks = rest[: len(columns)]
    rest = rest[len(columns) :]
    if started:
        carry_in, found_in = rest[:2]
        rest = rest[2:]
    held, carry_ref, found_ref, source_ref = rest
    chip = chip_ref[0]
    core = core_ref[0]
    x = x_ref[0]
    q_here = source_ref.shape[0]
    per_bits = per.bit_length() - 1
    near_bits = near.bit_length() - 1
    size = fine // 2 + 16
    blocks = [
        (stack, z * size, (chip ^ (z * near + column)) * 2 + (1 - core if other else core))
        for stack, (column, other) in zip(stacks, columns)
        for z in range(far)
    ]

    stations = entry_ref.shape[2]
    twice = (iota((stations, HALF), 0) == (iota((stations, HALF), 1) >> 1)).astype(jnp.bfloat16)
    entries = jnp.concatenate(
        [
            jnp.dot(
                entry_ref[0, pl.ds((group * GROUP + c) ^ x, 1), :]
                .astype(jnp.float32)
                .astype(jnp.bfloat16),
                twice,
                preferred_element_type=jnp.float32,
            )
            for c in range(GROUP)
        ],
        axis=1,
    ).astype(jnp.int32)
    row = iota((2 * LANES, LANES), 0)
    weight = jnp.where(row < LANES, 2.0**-8, 2.0**-16)
    spread = jnp.concatenate(
        [
            jnp.where(
                ((row & (HALF - 1)) == entries) & (((row >> 6) & 1) == half), weight, 0.0
            ).astype(jnp.bfloat16)
            for half in range(2)
        ],
        axis=1,
    )
    code = jnp.concatenate([stack[at : at + fine // 2, :] for stack, at, _ in blocks], axis=0)
    code = code.astype(jnp.int32).astype(jnp.float32)
    high = jnp.floor(code * (1.0 / 256.0))
    digits = jnp.concatenate([high, code - 256.0 * high], axis=1).astype(jnp.bfloat16)
    turns = jnp.dot(digits, spread, preferred_element_type=jnp.float32)
    for index, (_, _, owner) in enumerate(blocks):
        for half in range(2):
            at = (owner * 2 + half) * (fine // 2) * pitch + pitch - 1
            held[pl.ds(at, fine // 2, stride=pitch), :] = turns[
                index * (fine // 2) : (index + 1) * (fine // 2), half * LANES : (half + 1) * LANES
            ]

    if started:
        carry = carry_in[:, 0:1]
        found = found_in[...]
    else:
        carry = jnp.zeros((q_here, 1), jnp.float32)
        found = jnp.zeros((2 * q_here, LANES), jnp.float32)
    lane = iota((q_here, fine), 1)
    hits = []
    for stack, at, _ in blocks:
        tail = stack[at + fine // 2 : at + size, :].astype(jnp.int32)
        bins = jnp.concatenate([tail[r : r + 1, :] for r in range(fine // LANES)], axis=1)
        bin_owner = bins >> per_bits
        relative = (bin_owner >> 1) ^ chip
        label = ((relative & (near - 1)) * far + (relative >> near_bits)) * per
        label = label + (bins & (per - 1))
        label = jnp.where((bin_owner & 1) == core, label, -1)
        hits.append(jnp.where(iota((q_here, fine), 0) == label, 1.0, 0.0))
    above = (iota((fine, fine), 0) < iota((fine, fine), 1)).astype(jnp.bfloat16)
    every = jnp.concatenate(hits, axis=0).astype(jnp.bfloat16)
    every = jnp.dot(every, above, preferred_element_type=jnp.float32)
    ids, at_rank = [], []
    for index, (hit, (_, _, owner)) in enumerate(zip(hits, blocks)):
        before = every[index * q_here : (index + 1) * q_here]
        rank = jnp.sum(hit * (before + carry), axis=0, keepdims=True)
        carry = carry + before[:, fine - 1 : fine] + hit[:, fine - 1 : fine]
        at_rank.append((iota((LANES, fine), 0) == rank.astype(jnp.int32)).astype(jnp.bfloat16))
        high = hit * (owner * (fine // LANES) + (lane >> 7)).astype(jnp.float32)
        low = hit * (lane & (LANES - 1)).astype(jnp.float32)
        ids.append(jnp.concatenate([high, low], axis=0).astype(jnp.bfloat16))
    found = found + lax.dot_general(
        jnp.concatenate(ids, axis=1),
        jnp.concatenate(at_rank, axis=1),
        (((1,), (1,)), ((), ())),
        preferred_element_type=jnp.float32,
    )
    carry_ref[...] = jnp.broadcast_to(carry, carry_ref.shape)
    found_ref[...] = found
    source_ref[...] = ((found[:q_here] * LANES + found[q_here:]) * pitch).astype(jnp.int32)


def wave(z):
    value = jnp.full_like(z, COSINE[-1])
    for coefficient in COSINE[-2::-1]:
        value = value * z + coefficient
    return value


def correlate_kernel(source_ref, held, *rest, first_pair, pairs, spectra, sent):
    outs = rest[: 1 if sent else GROUP]
    rest = rest[len(outs) :]
    even, odd, wide_even, wide_odd, kept = rest[:5]
    sums = rest[5:] if sent else outs

    def gather(unit, into):
        for first in range(0, LANES, 32):
            at = [source_ref[unit, first + k] for k in range(32)]
            rows = [held[pl.ds(a, ROW), :] for a in at]
            for k in range(32):
                into[(first + k) * ROW : (first + k + 1) * ROW, :] = rows[k]

    upper = (iota((HALF, LANES), 1) & (HALF - 1)) > iota((HALF, LANES), 0)
    left = iota((HALF, LANES), 1) < HALF

    def rotate(rows, wide):
        turns = rows[pl.ds(2 * spectra, LANES, stride=ROW), :].T
        turning = []
        for centre in range(GROUP):
            angle = turns[centre * HALF : (centre + 1) * HALF]
            cosine = jnp.abs(angle) - 0.5
            sine = jnp.abs(angle - 0.25) - 0.5
            turning.append((wave(cosine * cosine), wave(sine * sine)))
        for t in range(2 * spectra):
            volts = rows[pl.ds(t, LANES, stride=ROW), :].T
            real, imaginary = volts[:HALF], volts[HALF:]
            columns = slice(t * LANES, (t + 1) * LANES)
            for centre in range(GROUP):
                cosine, sine = turning[centre]
                rotated = (real * cosine + imaginary * sine, imaginary * cosine - real * sine)
                for part, value in enumerate(rotated):
                    coarse = value.astype(jnp.bfloat16)
                    rest_of = (value - coarse.astype(jnp.float32)).astype(jnp.bfloat16)
                    wide[centre, part * HALF : (part + 1) * HALF, columns] = coarse
                    wide[centre, LANES + part * HALF : LANES + (part + 1) * HALF, columns] = rest_of

    def correlate(wide):
        results = []
        for centre in range(GROUP):
            product = lax.dot_general(
                wide[centre],
                wide[centre, :LANES],
                (((1,), (1,)), ((), ())),
                preferred_element_type=jnp.float32,
            )
            product = product[:LANES] + product[LANES:]
            under = pltpu.roll(product[HALF:], HALF, 1)
            results.append(product[:HALF] + jnp.where(left, under, -under))
        return results

    def emit(pair, seconds):
        for centre in range(GROUP):
            first, second = kept[centre], seconds[centre]
            first = jnp.where(upper, first, pltpu.roll(first, HALF, 1))
            second = jnp.where(upper, pltpu.roll(second, HALF, 1), second)
            value = jnp.where(left, first, second)
            at = pl.ds(pl.multiple_of(pair * HALF, HALF), HALF)
            sums[centre][at, :] = value

    base = 2 * first_pair
    last = base + 2 * pairs - 1
    gather(base, even)

    def one(pair, _):
        unit = base + 2 * pair
        gather(unit + 1, odd)
        rotate(even, wide_even)
        emit(jnp.maximum(pair - 1, 0), correlate(wide_odd))
        gather(jnp.minimum(unit + 2, last), even)
        rotate(odd, wide_odd)
        for centre, value in enumerate(correlate(wide_even)):
            kept[centre] = value
        return 0

    lax.fori_loop(0, pairs, one, 0)
    emit(pairs - 1, correlate(wide_odd))
    if sent:
        for centre in range(GROUP):
            for pair in range(pairs):
                at = slice(pair * HALF, (pair + 1) * HALF)
                outs[0][centre, at, :] = encode(sums[centre][at, :])


def join_kernel(*refs, arrivals):
    owns, arrived, outs = refs[:GROUP], refs[GROUP : GROUP + arrivals], refs[GROUP + arrivals :]
    for at in range(0, owns[0].shape[0], HALF):
        for c in range(GROUP):
            value = owns[c][at : at + HALF, :]
            for ref in arrived:
                value = value + decode(ref[c, at : at + HALF, :])
            outs[c][at : at + HALF, :] = encode(value) if outs[c].dtype == jnp.int16 else value


def merge_kernel(own_ref, *refs, arrivals, far, pairs):
    own_out = refs[arrivals]
    outs = refs[arrivals + 1 :]
    for z in range(far):
        for pair in range(pairs):
            at = pl.ds((z * pairs + pair) * HALF, HALF)
            total = own_ref[at, :]
            for ref in refs[:arrivals]:
                total = total + decode(ref[at, :])
            to = pl.ds(pair * HALF, HALF)
            if z == 0:
                own_out[to, :] = total
            else:
                outs[z - 1][to, :] = encode(total)


def finish_kernel(members_ref, own_ref, *refs, arrivals, pairs, scale):
    out_ref = refs[arrivals]
    baselines = members_ref.shape[1]
    first = members_ref[0:1, :]
    second = members_ref[1:2, :]
    rising = first < second
    station = iota((HALF, baselines), 0)
    for pair in range(pairs):
        at = pl.ds(pair * HALF, HALF)
        total = own_ref[at, :]
        for ref in refs[:arrivals]:
            total = total + decode(ref[at, :])
        total = total * scale
        total = jnp.where(iota(total.shape, 0) < 60, total, 0.0)
        flipped = total.T
        coarse = flipped.astype(jnp.bfloat16)
        medium = (flipped - coarse.astype(jnp.float32)).astype(jnp.bfloat16)
        stack = jnp.concatenate([coarse, medium], axis=0)
        picked = {}
        for side, members in enumerate((first, second)):
            for p in range(2):
                choose = (station == 2 * members + p).astype(jnp.bfloat16)
                rows = jnp.dot(stack, choose, preferred_element_type=jnp.float32)
                rows = rows[:LANES] + rows[LANES:]
                partner = second if side == 0 else first
                for half in range(2):
                    for p2 in range(2):
                        match = station == 2 * partner + p2
                        part = rows[half * HALF : (half + 1) * HALF]
                        picked[side, half, p, p2] = jnp.sum(
                            jnp.where(match, part, 0.0), axis=0, keepdims=True
                        )
        for half in range(2):
            real, imaginary = [], []
            for p in range(2):
                for p2 in range(2):
                    a = picked[0, half, p, p2]
                    b = picked[1, half, p2, p]
                    real.append(jnp.where(rising, a, b))
                    imaginary.append(jnp.where(rising, b, -a))
            out_ref[2 * pair + half, 0] = jnp.concatenate(real, axis=0)
            out_ref[2 * pair + half, 1] = jnp.concatenate(imaginary, axis=0)


def on_device(volts, entry, turning, members, target, *, tm, chips):
    near = max(1, chips // 4)
    far = chips // near
    fine = turning.shape[1]
    spectra = volts.shape[1]
    centres = entry.shape[1]
    per_device = Q // (2 * chips)
    pairs = per_device // 2
    channels = volts.shape[4]

    def across_chips(x, step):
        return lax.ppermute(x, "chip", [(i, i ^ step) for i in range(chips)])

    def across_cores(x):
        return lax.ppermute(x, "core", [(0, 1), (1, 0)])

    chip = lax.axis_index("chip")
    core = lax.axis_index("core")
    x = lax.axis_index("tm")
    place = [value.astype(jnp.int32).reshape(1) for value in (chip, core, x)]
    other = across_cores(volts)
    block = pl.pallas_call(
        pack_kernel,
        in_specs=[HBM, HBM],
        out_specs=VMEM,
        out_shape=jax.ShapeDtypeStruct((fine // 2 + 16, LANES), jnp.int16),
        scratch_shapes=[
            pltpu.VMEM(turning.shape, jnp.float32),
            pltpu.VMEM((fine // LANES, LANES), jnp.int32),
            pltpu.SemaphoreType.DMA((2,)),
        ],
        compiler_params=params(56),
        cost_estimate=cost(1),
        name="pack",
    )(turning, target.reshape(fine // LANES, LANES))
    line = [block] + [across_chips(block, z * near) for z in range(1, far)]

    pitch = 2 * spectra + 1
    held_type = pltpu.VMEM((channels * pitch + ROW, LANES), jnp.float32)

    def rows(side, *operands):
        return pl.pallas_call(
            functools.partial(rows_kernel, first=side * spectra, pitch=pitch),
            in_specs=[HBM, SMEM, SMEM, SMEM, VMEM][: 4 + side],
            out_specs=VMEM,
            out_shape=held_type,
            scratch_shapes=[
                pltpu.VMEM((channels // WIDTH, 2, spectra, 32, 2, WIDTH), jnp.bfloat16),
                pltpu.SemaphoreType.DMA((channels // WIDTH,)),
            ],
            input_output_aliases={4: 0} if side else {},
            compiler_params=params(40),
            cost_estimate=cost(5),
            name="rows",
        )(*operands)

    held = rows(0, volts, *place)
    size = block.shape[0]
    stack = pl.pallas_call(
        stack_kernel,
        in_specs=[ANY] + [VMEM] * far,
        out_specs=VMEM,
        out_shape=jax.ShapeDtypeStruct((far * size, LANES), jnp.int16),
        compiler_params=params(4),
        cost_estimate=cost(1),
        name="stack",
    )(held, *line)
    mine = [stack] + [across_chips(stack, y) for y in range(1, near)]
    theirs = [across_cores(stack)]
    held = rows(1, other, *place, held)
    each = far * pairs
    arrived = []
    after = entry
    for group in range(centres // GROUP):
        state = ()
        for part in range(3 if near > 1 else 1):
            if part == 0:
                columns = [(0, False), (0, True)]
            else:
                columns = [(y, part == 2) for y in range(1, near)]
            if part == 1 and group == 0:
                state, mine = lax.optimization_barrier((state, mine))
                theirs += [across_cores(value) for value in mine[1:]]
            stacks = [(theirs if across else mine)[y] for y, across in columns]
            held, *state, source = pl.pallas_call(
                functools.partial(
                    prepare_kernel,
                    columns=columns,
                    started=part > 0,
                    group=group,
                    near=near,
                    far=far,
                    per=per_device,
                    fine=fine,
                    pitch=pitch,
                ),
                in_specs=[SMEM, SMEM, SMEM, VMEM, ANY] + [VMEM] * (1 + len(stacks) + len(state)),
                out_specs=[VMEM] * 4,
                out_shape=[
                    held_type,
                    jax.ShapeDtypeStruct((Q // 2, LANES), jnp.float32),
                    jax.ShapeDtypeStruct((Q, LANES), jnp.float32),
                    jax.ShapeDtypeStruct((Q // 2, LANES), jnp.int32),
                ],
                input_output_aliases={5: 0},
                compiler_params=params(16),
                cost_estimate=cost(2),
                name="prepare",
            )(*place, entry, after, held, *stacks, *state)
        def correlate(first_pair, out_types, source=source, held=held):
            return pl.pallas_call(
                functools.partial(
                    correlate_kernel,
                    first_pair=first_pair,
                    pairs=each,
                    spectra=spectra,
                    sent=len(out_types) == 1,
                ),
                in_specs=[SMEM, VMEM],
                out_specs=[VMEM] * len(out_types),
                out_shape=out_types,
                scratch_shapes=[
                    pltpu.VMEM((LANES * ROW + ROW, LANES), jnp.float32),
                    pltpu.VMEM((LANES * ROW + ROW, LANES), jnp.float32),
                    pltpu.VMEM((GROUP, 2 * LANES, 2 * spectra * LANES), jnp.bfloat16),
                    pltpu.VMEM((GROUP, 2 * LANES, 2 * spectra * LANES), jnp.bfloat16),
                    pltpu.VMEM((GROUP, HALF, LANES), jnp.float32),
                ]
                + [pltpu.VMEM((each * HALF, LANES), jnp.float32)] * (GROUP if len(out_types) == 1 else 0),
                compiler_params=params(12),
                cost_estimate=cost(9),
                name="correlate",
            )(source, held)

        columns_in = []
        for y in range(1, near):
            sent = correlate(
                y * each, [jax.ShapeDtypeStruct((GROUP, each * HALF, LANES), jnp.int16)]
            )[0]
            columns_in.append(across_chips(sent, y))
        own = correlate(0, [jax.ShapeDtypeStruct((each * HALF, LANES), jnp.float32)] * GROUP)
        after = own[0]
        if columns_in:
            kinds = [jnp.int16 if group + c else jnp.float32 for c in range(GROUP)]
            own = pl.pallas_call(
                functools.partial(join_kernel, arrivals=len(columns_in)),
                in_specs=[VMEM] * (GROUP + len(columns_in)),
                out_specs=[VMEM] * GROUP,
                out_shape=[jax.ShapeDtypeStruct((each * HALF, LANES), kind) for kind in kinds],
                compiler_params=params(8),
                cost_estimate=cost(1),
                name="join",
            )(*own, *columns_in)
        for c in range(GROUP):
            centre = group * GROUP + c
            if centre == 0:
                total = own[c]
            else:
                arrived.append(
                    lax.ppermute(own[c], "tm", [(i, i ^ centre) for i in range(tm)])
                )
    rows = pairs * HALF
    merged = pl.pallas_call(
        functools.partial(merge_kernel, arrivals=len(arrived), far=far, pairs=pairs),
        in_specs=[VMEM] * (1 + len(arrived)),
        out_specs=[VMEM] * far,
        out_shape=[
            jax.ShapeDtypeStruct((rows, LANES), jnp.int16 if z else jnp.float32)
            for z in range(far)
        ],
        compiler_params=params(6),
        cost_estimate=cost(1),
        name="merge",
    )(total, *arrived)
    final = [across_chips(merged[z], z * near) for z in range(far - 1, 0, -1)]
    return pl.pallas_call(
        functools.partial(finish_kernel, arrivals=len(final), pairs=pairs, scale=Q / channels),
        in_specs=[VMEM] * (2 + len(final)),
        out_specs=VMEM,
        out_shape=jax.ShapeDtypeStruct((per_device, 2, 4, members.shape[0]), jnp.float32),
        compiler_params=params(6),
        cost_estimate=cost(2),
        name="finish",
    )(members.T, merged[0], *final)


def solution(mesh):
    tm = mesh.shape["tm"]
    chips = mesh.shape["chan"] // 2
    inner = Mesh(mesh.devices.reshape(tm, chips, 2), ("tm", "chip", "core"))
    every = ("tm", "chip", "core")
    split = ("chip", "core")
    return jax.shard_map(
        functools.partial(on_device, tm=tm, chips=chips),
        mesh=inner,
        in_specs=(
            P(None, every, None, None, None),
            P("tm", None, None),
            P(None, split),
            P(),
            P(split),
        ),
        out_specs=P(every, None, None, None),
        check_vma=False,
    )
```

```python
import functools

import jax
import jax.numpy as jnp
import numpy as np
from jax import lax
from jax.experimental import pallas as pl
from jax.experimental.pallas import tpu as pltpu
from jax.sharding import Mesh
from jax.sharding import PartitionSpec as P

Q = 64
LANES = 128
HALF = 64
WIDTH = 1024
ROW = 8
GROUP = 2
TURN = 65536.0
COSINE = (-0.9999992251396179, 19.738981246948242, -64.92865753173828, 85.27162170410156, -58.79049301147461, 21.07110595703125)
VMEM = pl.BlockSpec(memory_space=pltpu.VMEM)
SMEM = pl.BlockSpec(memory_space=pltpu.SMEM)
ANY = pl.BlockSpec(memory_space=pl.ANY)
HBM = pl.BlockSpec(memory_space=pltpu.HBM)


def iota(shape, dim):
    return lax.broadcasted_iota(jnp.int32, shape, dim)


def params(mib):
    return pltpu.CompilerParams(vmem_limit_bytes=mib * 1024 * 1024)


def cost(microseconds):
    return pl.CostEstimate(
        flops=int(microseconds * 1.0e9), bytes_accessed=int(microseconds * 3.0e6), transcendentals=0
    )


def pack_kernel(turning_hbm, bins_hbm, out_ref, turning_ref, bins_ref, sems):
    entries, fine = turning_ref.shape
    rows = fine // 2
    copies = [
        pltpu.make_async_copy(turning_hbm, turning_ref, sems.at[0]),
        pltpu.make_async_copy(bins_hbm, bins_ref, sems.at[1]),
    ]
    for copy in copies:
        copy.start()
    for copy in copies:
        copy.wait()
    codes = jnp.round(turning_ref[...] * (TURN / (2.0 * np.pi)))
    flipped = codes.T
    pair = jnp.concatenate([flipped[:rows], flipped[rows:]], axis=1)
    out_ref[0:rows, :] = pair.astype(jnp.int32).astype(jnp.int16)
    spare = jnp.zeros((out_ref.shape[0] - rows - bins_ref.shape[0], LANES), jnp.int32)
    out_ref[rows:, :] = jnp.concatenate([bins_ref[...], spare], axis=0).astype(jnp.int16)


def stack_kernel(after_ref, *refs):
    del after_ref
    out_ref = refs[-1]
    size = refs[0].shape[0]
    for k, ref in enumerate(refs[:-1]):
        out_ref[k * size : (k + 1) * size, :] = ref[...]


def encode(block):
    top = jnp.max(jnp.max(jnp.abs(block), axis=0, keepdims=True), axis=1, keepdims=True)
    power = jnp.floor(jnp.log2(jnp.maximum(top, 1e-30)))
    code = jnp.clip(jnp.round(block * jnp.exp2(14.0 - power)), -32767.0, 32767.0)
    code = jnp.where(iota(block.shape, 0) == 60, power, code)
    return code.astype(jnp.int32).astype(jnp.int16)


def decode(code):
    code = code.astype(jnp.int32).astype(jnp.float32)
    scale = jnp.exp2(code[60:61, 0:1] - 14.0)
    return code * scale


def rows_kernel(volts_ref, *rest, first, pitch):
    held, raw, sems = rest[-3:]
    parts, spectra, stations = volts_ref.shape[:3]
    width = raw.shape[-1]
    steps = raw.shape[0]
    unroll = 2

    def fetch(step):
        return pltpu.make_async_copy(
            volts_ref.at[:, :, :, :, pl.ds(pl.multiple_of(step * width, width), width)],
            raw.at[step, :, :, pl.ds(0, stations)],
            sems.at[step],
        )

    def start(step, _):
        raw[step, :, :, stations:] = jnp.zeros(
            (parts, spectra, raw.shape[3] - stations, 2, width), jnp.bfloat16
        )
        fetch(step).start()
        return 0

    lax.fori_loop(0, steps, start, 0)

    def flip(group, _):
        for unit in range(unroll):
            fetch(group * unroll + unit).wait()
        for unit in range(unroll):
            step = group * unroll + unit
            for k in range(width // LANES):
                block = raw[step, :, :, :, :, k * LANES : (k + 1) * LANES]
                block = block.reshape(parts * spectra * HALF, LANES)
                for t in range(spectra):
                    both = jnp.concatenate(
                        [
                            block[(part * spectra + t) * HALF : (part * spectra + t + 1) * HALF]
                            for part in range(parts)
                        ],
                        axis=0,
                    )
                    at = (step * width + k * LANES) * pitch + first + t
                    held[pl.ds(at, LANES, stride=pitch), :] = both.astype(jnp.float32).T
        return 0

    lax.fori_loop(0, steps // unroll, flip, 0)


def prepare_kernel(
    chip_ref, core_ref, x_ref, entry_ref, after_ref, held_in, *rest, columns, started, group, near, far, per, fine, pitch
):
    del after_ref, held_in
    stacks = rest[: len(columns)]
    rest = rest[len(columns) :]
    if started:
        carry_in, found_in = rest[:2]
        rest = rest[2:]
    held, carry_ref, found_ref, source_ref = rest
    chip = chip_ref[0]
    core = core_ref[0]
    x = x_ref[0]
    q_here = source_ref.shape[0]
    per_bits = per.bit_length() - 1
    near_bits = near.bit_length() - 1
    size = fine // 2 + 16
    blocks = [
        (stack, z * size, (chip ^ (z * near + column)) * 2 + (1 - core if other else core))
        for stack, (column, other) in zip(stacks, columns)
        for z in range(far)
    ]

    stations = entry_ref.shape[2]
    twice = (iota((stations, HALF), 0) == (iota((stations, HALF), 1) >> 1)).astype(jnp.bfloat16)
    entries = jnp.concatenate(
        [
            jnp.dot(
                entry_ref[0, pl.ds((group * GROUP + c) ^ x, 1), :]
                .astype(jnp.float32)
                .astype(jnp.bfloat16),
                twice,
                preferred_element_type=jnp.float32,
            )
            for c in range(GROUP)
        ],
        axis=1,
    ).astype(jnp.int32)
    row = iota((2 * LANES, LANES), 0)
    weight = jnp.where(row < LANES, 2.0**-8, 2.0**-16)
    spread = jnp.concatenate(
        [
            jnp.where(
                ((row & (HALF - 1)) == entries) & (((row >> 6) & 1) == half), weight, 0.0
            ).astype(jnp.bfloat16)
            for half in range(2)
        ],
        axis=1,
    )
    code = jnp.concatenate([stack[at : at + fine // 2, :] for stack, at, _ in blocks], axis=0)
    code = code.astype(jnp.int32).astype(jnp.float32)
    high = jnp.floor(code * (1.0 / 256.0))
    digits = jnp.concatenate([high, code - 256.0 * high], axis=1).astype(jnp.bfloat16)
    turns = jnp.dot(digits, spread, preferred_element_type=jnp.float32)
    for index, (_, _, owner) in enumerate(blocks):
        for half in range(2):
            at = (owner * 2 + half) * (fine // 2) * pitch + pitch - 1
            held[pl.ds(at, fine // 2, stride=pitch), :] = turns[
                index * (fine // 2) : (index + 1) * (fine // 2), half * LANES : (half + 1) * LANES
            ]

    if started:
        carry = carry_in[:, 0:1]
        found = found_in[...]
    else:
        carry = jnp.zeros((q_here, 1), jnp.float32)
        found = jnp.zeros((2 * q_here, LANES), jnp.float32)
    lane = iota((q_here, fine), 1)
    hits = []
    for stack, at, _ in blocks:
        tail = stack[at + fine // 2 : at + size, :].astype(jnp.int32)
        bins = jnp.concatenate([tail[r : r + 1, :] for r in range(fine // LANES)], axis=1)
        bin_owner = bins >> per_bits
        relative = (bin_owner >> 1) ^ chip
        label = ((relative & (near - 1)) * far + (relative >> near_bits)) * per
        label = label + (bins & (per - 1))
        label = jnp.where((bin_owner & 1) == core, label, -1)
        hits.append(jnp.where(iota((q_here, fine), 0) == label, 1.0, 0.0))
    above = (iota((fine, fine), 0) < iota((fine, fine), 1)).astype(jnp.bfloat16)
    every = jnp.concatenate(hits, axis=0).astype(jnp.bfloat16)
    every = jnp.dot(every, above, preferred_element_type=jnp.float32)
    ids, at_rank = [], []
    for index, (hit, (_, _, owner)) in enumerate(zip(hits, blocks)):
        before = every[index * q_here : (index + 1) * q_here]
        rank = jnp.sum(hit * (before + carry), axis=0, keepdims=True)
        carry = carry + before[:, fine - 1 : fine] + hit[:, fine - 1 : fine]
        at_rank.append((iota((LANES, fine), 0) == rank.astype(jnp.int32)).astype(jnp.bfloat16))
        high = hit * (owner * (fine // LANES) + (lane >> 7)).astype(jnp.float32)
        low = hit * (lane & (LANES - 1)).astype(jnp.float32)
        ids.append(jnp.concatenate([high, low], axis=0).astype(jnp.bfloat16))
    found = found + lax.dot_general(
        jnp.concatenate(ids, axis=1),
        jnp.concatenate(at_rank, axis=1),
        (((1,), (1,)), ((), ())),
        preferred_element_type=jnp.float32,
    )
    carry_ref[...] = jnp.broadcast_to(carry, carry_ref.shape)
    found_ref[...] = found
    source_ref[...] = ((found[:q_here] * LANES + found[q_here:]) * pitch).astype(jnp.int32)


def wave(z):
    value = jnp.full_like(z, COSINE[-1])
    for coefficient in COSINE[-2::-1]:
        value = value * z + coefficient
    return value


def correlate_kernel(source_ref, held, *rest, first_pair, pairs, spectra, sent):
    outs = rest[: 1 if sent else GROUP]
    rest = rest[len(outs) :]
    even, odd, wide_even, wide_odd, kept = rest[:5]
    sums = rest[5:] if sent else outs

    def gather(unit, into):
        for first in range(0, LANES, 32):
            at = [source_ref[unit, first + k] for k in range(32)]
            rows = [held[pl.ds(a, ROW), :] for a in at]
            for k in range(32):
                into[(first + k) * ROW : (first + k + 1) * ROW, :] = rows[k]

    upper = (iota((HALF, LANES), 1) & (HALF - 1)) > iota((HALF, LANES), 0)
    left = iota((HALF, LANES), 1) < HALF

    def rotate(rows, wide):
        turns = rows[pl.ds(2 * spectra, LANES, stride=ROW), :].T
        turning = []
        for centre in range(GROUP):
            angle = turns[centre * HALF : (centre + 1) * HALF]
            cosine = jnp.abs(angle) - 0.5
            sine = jnp.abs(angle - 0.25) - 0.5
            turning.append((wave(cosine * cosine), wave(sine * sine)))
        for t in range(2 * spectra):
            volts = rows[pl.ds(t, LANES, stride=ROW), :].T
            real, imaginary = volts[:HALF], volts[HALF:]
            columns = slice(t * LANES, (t + 1) * LANES)
            for centre in range(GROUP):
                cosine, sine = turning[centre]
                rotated = (real * cosine + imaginary * sine, imaginary * cosine - real * sine)
                for part, value in enumerate(rotated):
                    coarse = value.astype(jnp.bfloat16)
                    rest_of = (value - coarse.astype(jnp.float32)).astype(jnp.bfloat16)
                    wide[centre, part * HALF : (part + 1) * HALF, columns] = coarse
                    wide[centre, LANES + part * HALF : LANES + (part + 1) * HALF, columns] = rest_of

    def correlate(wide):
        results = []
        for centre in range(GROUP):
            product = lax.dot_general(
                wide[centre],
                wide[centre, :LANES],
                (((1,), (1,)), ((), ())),
                preferred_element_type=jnp.float32,
            )
            product = product[:LANES] + product[LANES:]
            under = pltpu.roll(product[HALF:], HALF, 1)
            results.append(product[:HALF] + jnp.where(left, under, -under))
        return results

    def emit(pair, seconds):
        for centre in range(GROUP):
            first, second = kept[centre], seconds[centre]
            first = jnp.where(upper, first, pltpu.roll(first, HALF, 1))
            second = jnp.where(upper, pltpu.roll(second, HALF, 1), second)
            value = jnp.where(left, first, second)
            at = pl.ds(pl.multiple_of(pair * HALF, HALF), HALF)
            sums[centre][at, :] = value

    base = 2 * first_pair
    last = base + 2 * pairs - 1
    gather(base, even)

    def one(pair, _):
        unit = base + 2 * pair
        gather(unit + 1, odd)
        rotate(even, wide_even)
        emit(jnp.maximum(pair - 1, 0), correlate(wide_odd))
        gather(jnp.minimum(unit + 2, last), even)
        rotate(odd, wide_odd)
        for centre, value in enumerate(correlate(wide_even)):
            kept[centre] = value
        return 0

    lax.fori_loop(0, pairs, one, 0)
    emit(pairs - 1, correlate(wide_odd))
    if sent:
        for centre in range(GROUP):
            for pair in range(pairs):
                at = slice(pair * HALF, (pair + 1) * HALF)
                outs[0][centre, at, :] = encode(sums[centre][at, :])


def join_kernel(*refs, arrivals):
    owns, arrived, outs = refs[:GROUP], refs[GROUP : GROUP + arrivals], refs[GROUP + arrivals :]
    for at in range(0, owns[0].shape[0], HALF):
        for c in range(GROUP):
            value = owns[c][at : at + HALF, :]
            for ref in arrived:
                value = value + decode(ref[c, at : at + HALF, :])
            outs[c][at : at + HALF, :] = encode(value) if outs[c].dtype == jnp.int16 else value


def merge_kernel(own_ref, *refs, arrivals, far, pairs):
    own_out = refs[arrivals]
    outs = refs[arrivals + 1 :]
    for z in range(far):
        for pair in range(pairs):
            at = pl.ds((z * pairs + pair) * HALF, HALF)
            total = own_ref[at, :]
            for ref in refs[:arrivals]:
                total = total + decode(ref[at, :])
            to = pl.ds(pair * HALF, HALF)
            if z == 0:
                own_out[to, :] = total
            else:
                outs[z - 1][to, :] = encode(total)


def finish_kernel(members_ref, own_ref, *refs, arrivals, pairs, scale):
    out_ref = refs[arrivals]
    baselines = members_ref.shape[1]
    first = members_ref[0:1, :]
    second = members_ref[1:2, :]
    rising = first < second
    station = iota((HALF, baselines), 0)
    stacks = []
    for pair in range(pairs):
        at = pl.ds(pair * HALF, HALF)
        total = own_ref[at, :]
        for ref in refs[:arrivals]:
            total = total + decode(ref[at, :])
        total = total * scale
        total = jnp.where(iota(total.shape, 0) < 60, total, 0.0)
        flipped = total.T
        coarse = flipped.astype(jnp.bfloat16)
        medium = (flipped - coarse.astype(jnp.float32)).astype(jnp.bfloat16)
        stacks += [coarse, medium]
    stack = jnp.concatenate(stacks, axis=0)
    picked = {}
    for side, members in enumerate((first, second)):
        partner = second if side == 0 else first
        for p in range(2):
            choose = (station == 2 * members + p).astype(jnp.bfloat16)
            rows = jnp.dot(stack, choose, preferred_element_type=jnp.float32)
            for pair in range(pairs):
                base = pair * 2 * LANES
                both = rows[base : base + LANES] + rows[base + LANES : base + 2 * LANES]
                for half in range(2):
                    for p2 in range(2):
                        match = station == 2 * partner + p2
                        part = both[half * HALF : (half + 1) * HALF]
                        picked[pair, side, half, p, p2] = jnp.sum(
                            jnp.where(match, part, 0.0), axis=0, keepdims=True
                        )
    for pair in range(pairs):
        for half in range(2):
            real, imaginary = [], []
            for p in range(2):
                for p2 in range(2):
                    a = picked[pair, 0, half, p, p2]
                    b = picked[pair, 1, half, p2, p]
                    real.append(jnp.where(rising, a, b))
                    imaginary.append(jnp.where(rising, b, -a))
            out_ref[2 * pair + half, 0] = jnp.concatenate(real, axis=0)
            out_ref[2 * pair + half, 1] = jnp.concatenate(imaginary, axis=0)


def on_device(volts, entry, turning, members, target, *, tm, chips):
    near = max(1, chips // 4)
    far = chips // near
    fine = turning.shape[1]
    spectra = volts.shape[1]
    centres = entry.shape[1]
    per_device = Q // (2 * chips)
    pairs = per_device // 2
    channels = volts.shape[4]

    def across_chips(x, step):
        return lax.ppermute(x, "chip", [(i, i ^ step) for i in range(chips)])

    def across_cores(x):
        return lax.ppermute(x, "core", [(0, 1), (1, 0)])

    chip = lax.axis_index("chip")
    core = lax.axis_index("core")
    x = lax.axis_index("tm")
    place = [value.astype(jnp.int32).reshape(1) for value in (chip, core, x)]
    other = across_cores(volts)
    block = pl.pallas_call(
        pack_kernel,
        in_specs=[HBM, HBM],
        out_specs=VMEM,
        out_shape=jax.ShapeDtypeStruct((fine // 2 + 16, LANES), jnp.int16),
        scratch_shapes=[
            pltpu.VMEM(turning.shape, jnp.float32),
            pltpu.VMEM((fine // LANES, LANES), jnp.int32),
            pltpu.SemaphoreType.DMA((2,)),
        ],
        compiler_params=params(56),
        cost_estimate=cost(1),
        name="pack",
    )(turning, target.reshape(fine // LANES, LANES))
    line = [block] + [across_chips(block, z * near) for z in range(1, far)]

    pitch = 2 * spectra + 1
    held_type = pltpu.VMEM((channels * pitch + ROW, LANES), jnp.float32)

    def rows(side, *operands):
        return pl.pallas_call(
            functools.partial(rows_kernel, first=side * spectra, pitch=pitch),
            in_specs=[HBM, SMEM, SMEM, SMEM, VMEM][: 4 + side],
            out_specs=VMEM,
            out_shape=held_type,
            scratch_shapes=[
                pltpu.VMEM((channels // WIDTH, 2, spectra, 32, 2, WIDTH), jnp.bfloat16),
                pltpu.SemaphoreType.DMA((channels // WIDTH,)),
            ],
            input_output_aliases={4: 0} if side else {},
            compiler_params=params(40),
            cost_estimate=cost(5),
            name="rows",
        )(*operands)

    held = rows(0, volts, *place)
    size = block.shape[0]
    stack = pl.pallas_call(
        stack_kernel,
        in_specs=[ANY] + [VMEM] * far,
        out_specs=VMEM,
        out_shape=jax.ShapeDtypeStruct((far * size, LANES), jnp.int16),
        compiler_params=params(4),
        cost_estimate=cost(1),
        name="stack",
    )(held, *line)
    mine = [stack] + [across_chips(stack, y) for y in range(1, near)]
    theirs = [across_cores(stack)]
    held = rows(1, other, *place, held)
    each = far * pairs
    arrived = []
    after = entry
    for group in range(centres // GROUP):
        state = ()
        for part in range(3 if near > 1 else 1):
            if part == 0:
                columns = [(0, False), (0, True)]
            else:
                columns = [(y, part == 2) for y in range(1, near)]
            if part == 1 and group == 0:
                state, mine = lax.optimization_barrier((state, mine))
                theirs += [across_cores(value) for value in mine[1:]]
            stacks = [(theirs if across else mine)[y] for y, across in columns]
            held, *state, source = pl.pallas_call(
                functools.partial(
                    prepare_kernel,
                    columns=columns,
                    started=part > 0,
                    group=group,
                    near=near,
                    far=far,
                    per=per_device,
                    fine=fine,
                    pitch=pitch,
                ),
                in_specs=[SMEM, SMEM, SMEM, VMEM, ANY] + [VMEM] * (1 + len(stacks) + len(state)),
                out_specs=[VMEM] * 4,
                out_shape=[
                    held_type,
                    jax.ShapeDtypeStruct((Q // 2, LANES), jnp.float32),
                    jax.ShapeDtypeStruct((Q, LANES), jnp.float32),
                    jax.ShapeDtypeStruct((Q // 2, LANES), jnp.int32),
                ],
                input_output_aliases={5: 0},
                compiler_params=params(16),
                cost_estimate=cost(2),
                name="prepare",
            )(*place, entry, after, held, *stacks, *state)
        def correlate(first_pair, out_types, source=source, held=held):
            return pl.pallas_call(
                functools.partial(
                    correlate_kernel,
                    first_pair=first_pair,
                    pairs=each,
                    spectra=spectra,
                    sent=len(out_types) == 1,
                ),
                in_specs=[SMEM, VMEM],
                out_specs=[VMEM] * len(out_types),
                out_shape=out_types,
                scratch_shapes=[
                    pltpu.VMEM((LANES * ROW + ROW, LANES), jnp.float32),
                    pltpu.VMEM((LANES * ROW + ROW, LANES), jnp.float32),
                    pltpu.VMEM((GROUP, 2 * LANES, 2 * spectra * LANES), jnp.bfloat16),
                    pltpu.VMEM((GROUP, 2 * LANES, 2 * spectra * LANES), jnp.bfloat16),
                    pltpu.VMEM((GROUP, HALF, LANES), jnp.float32),
                ]
                + [pltpu.VMEM((each * HALF, LANES), jnp.float32)] * (GROUP if len(out_types) == 1 else 0),
                compiler_params=params(12),
                cost_estimate=cost(9),
                name="correlate",
            )(source, held)

        columns_in = []
        for y in range(1, near):
            sent = correlate(
                y * each, [jax.ShapeDtypeStruct((GROUP, each * HALF, LANES), jnp.int16)]
            )[0]
            columns_in.append(across_chips(sent, y))
        own = correlate(0, [jax.ShapeDtypeStruct((each * HALF, LANES), jnp.float32)] * GROUP)
        after = own[0]
        if columns_in:
            kinds = [jnp.int16 if group + c else jnp.float32 for c in range(GROUP)]
            own = pl.pallas_call(
                functools.partial(join_kernel, arrivals=len(columns_in)),
                in_specs=[VMEM] * (GROUP + len(columns_in)),
                out_specs=[VMEM] * GROUP,
                out_shape=[jax.ShapeDtypeStruct((each * HALF, LANES), kind) for kind in kinds],
                compiler_params=params(8),
                cost_estimate=cost(1),
                name="join",
            )(*own, *columns_in)
        for c in range(GROUP):
            centre = group * GROUP + c
            if centre == 0:
                total = own[c]
            else:
                arrived.append(
                    lax.ppermute(own[c], "tm", [(i, i ^ centre) for i in range(tm)])
                )
    rows = pairs * HALF
    merged = pl.pallas_call(
        functools.partial(merge_kernel, arrivals=len(arrived), far=far, pairs=pairs),
        in_specs=[VMEM] * (1 + len(arrived)),
        out_specs=[VMEM] * far,
        out_shape=[
            jax.ShapeDtypeStruct((rows, LANES), jnp.int16 if z else jnp.float32)
            for z in range(far)
        ],
        compiler_params=params(6),
        cost_estimate=cost(1),
        name="merge",
    )(total, *arrived)
    final = [across_chips(merged[z], z * near) for z in range(far - 1, 0, -1)]
    return pl.pallas_call(
        functools.partial(finish_kernel, arrivals=len(final), pairs=pairs, scale=Q / channels),
        in_specs=[VMEM] * (2 + len(final)),
        out_specs=VMEM,
        out_shape=jax.ShapeDtypeStruct((per_device, 2, 4, members.shape[0]), jnp.float32),
        compiler_params=params(6),
        cost_estimate=cost(2),
        name="finish",
    )(members.T, merged[0], *final)


def solution(mesh):
    tm = mesh.shape["tm"]
    chips = mesh.shape["chan"] // 2
    inner = Mesh(mesh.devices.reshape(tm, chips, 2), ("tm", "chip", "core"))
    every = ("tm", "chip", "core")
    split = ("chip", "core")
    return jax.shard_map(
        functools.partial(on_device, tm=tm, chips=chips),
        mesh=inner,
        in_specs=(
            P(None, every, None, None, None),
            P("tm", None, None),
            P(None, split),
            P(),
            P(split),
        ),
        out_specs=P(every, None, None, None),
        check_vma=False,
    )
```
